32 devices in a mesh: rows: 8 (over z, x), seq: 4 (over y, core).
Axes of the slice: x: 2, y: 2, z: 4, core: 2. Of those that a mesh axis runs over, the one named last changes fastest.
Arguments:
- layer_in: bfloat16 [8, 1024, 1024], P('rows', 'seq'), may hold values from -6 to 6
- grad_out: bfloat16 [8, 1024, 1024], P('rows', 'seq'), may hold values from -6 to 6
- lengths: int32 [8], P('rows'), may hold values from 769 to 1024, as said below
- ln1_gain: bfloat16 [1024], P(('rows', 'seq')), may hold values from 0.5 to 1.5
- ln1_shift: bfloat16 [1024], P(('rows', 'seq')), may hold values from -1.1953125 to 1.1953125
- w_qkv: bfloat16 [1024, 3072], P(('rows', 'seq')), may hold values from -0.1875 to 0.1875
- b_qv: bfloat16 [2048], P(('rows', 'seq')), may hold values from -1.1953125 to 1.1953125
- w_out: bfloat16 [1024, 1024], P(('rows', 'seq')), may hold values from -0.75 to 0.75
- b_out: bfloat16 [1024], P(('rows', 'seq')), may hold values from -1.1953125 to 1.1953125
- ln2_gain: bfloat16 [1024], P(('rows', 'seq')), may hold values from 0.5 to 1.5
- ln2_shift: bfloat16 [1024], P(('rows', 'seq')), may hold values from -1.1953125 to 1.1953125
- w_fc1: bfloat16 [1024, 4096], P(('rows', 'seq')), may hold values from -0.1875 to 0.1875
- b_fc1: bfloat16 [4096], P(('rows', 'seq')), may hold values from -1.1953125 to 1.1953125
- w_fc2: bfloat16 [4096, 1024], P(('rows', 'seq')), may hold values from -0.09375 to 0.09375
- b_fc2: bfloat16 [1024], P(('rows', 'seq')), may hold values from -1.1953125 to 1.1953125
Outputs:
- layer_out: bfloat16 [8, 1024, 1024], P('rows', 'seq')
- grad_in: bfloat16 [8, 1024, 1024], P('rows', 'seq')
- grad_ln1_gain: float32 [1024], P(('rows', 'seq'))
- grad_ln1_shift: float32 [1024], P(('rows', 'seq'))
- grad_w_qkv: float32 [1024, 3072], P(('rows', 'seq'))
- grad_b_qv: float32 [2048], P(('rows', 'seq'))
- grad_w_out: float32 [1024, 1024], P(('rows', 'seq'))
- grad_b_out: float32 [1024], P(('rows', 'seq'))
- grad_ln2_gain: float32 [1024], P(('rows', 'seq'))
- grad_ln2_shift: float32 [1024], P(('rows', 'seq'))
- grad_w_fc1: float32 [1024, 4096], P(('rows', 'seq'))
- grad_b_fc1: float32 [4096], P(('rows', 'seq'))
- grad_w_fc2: float32 [4096, 1024], P(('rows', 'seq'))
- grad_b_fc2: float32 [1024], P(('rows', 'seq'))
The draws below stay inside these ranges and needn't reach their ends.
Inputs may be any that keep to these rules, and one draw needn't show every extreme that they name: Positions from lengths[s] on are padding; one sequence has exactly 1024 real tokens.
All inputs are finite; a program needn't handle non-finite values.
Results may differ from the reference program's by a relative error of at most 0.012.
Values may be sent and summed in bfloat16 or wider, within the bound.
No kernel may reach another device: no remote copies, remote signals or barrier semaphores. Data moves between devices by JAX's collectives and lax.ppermute only.
A program may use at most 256 MiB of HBM per device.

```python
import jax
import jax.numpy as jnp
from jax import lax

D = 1024
HEADS = 16
HD = 64
FF = 4096
LEN = 1024
LLOC = 256
SEQS = 8


def draw_lengths(key, part):
    key = jax.random.fold_in(key, 11)
    key_cut, key_pick = jax.random.split(key)
    shortfall = jax.random.randint(key_cut, (SEQS,), 0, LLOC)
    chosen = jax.random.randint(key_pick, (), 0, SEQS)
    seq_lengths = LEN - shortfall
    return jnp.where(jnp.arange(SEQS) == chosen, LEN, seq_lengths).astype(jnp.int32)


def steps_of(rng, dims, cuts, low, largest):
    loudness, own = 1.0, jax.random.fold_in(rng, 6)
    for dim, parts in cuts:
        steps = jnp.exp(jax.random.uniform(jax.random.fold_in(own, dim), (parts,), jnp.float32, low / len(cuts), largest / len(cuts)))
        loudness = loudness * jnp.repeat(steps, dims[dim] // parts).reshape([-1 if axis == dim else 1 for axis in range(len(dims))])
    return loudness


def noise(key, extent, deviation, bound, cuts=(), held_as=jnp.bfloat16):
    values = deviation * jax.random.normal(key, extent, jnp.float32)
    if cuts:
        values = values * steps_of(key, extent, cuts, -0.22, 0.18)
    return jnp.clip(values, -bound, bound).astype(held_as)


def setup_inputs(seed: int = 0) -> dict:
    key_list = jax.random.split(jax.random.key(seed), 16)
    layer_in = noise(key_list[0], (SEQS, LEN, D), 1.0, 6.0, ((0, 8), (1, 4)))
    grad_out = noise(key_list[1], (SEQS, LEN, D), 1.0, 6.0, ((0, 8), (1, 4)))
    lengths = draw_lengths(jax.random.fold_in(key_list[15], 71), 0)
    ln1_gain = jnp.clip(1.0 + 0.1 * jax.random.normal(key_list[3], (D,), jnp.float32), 0.5, 1.5).astype(jnp.bfloat16)
    ln1_shift = noise(key_list[4], (D,), 0.2, 1.1953125, ((0, 32),))
    w_qkv = noise(key_list[5], (D, 3 * D), D ** -0.5, 0.1875, ((0, 32),))
    b_qv = noise(key_list[6], (2 * D,), 0.2, 1.1953125, ((0, 32),))
    w_out = noise(key_list[7], (D, D), (D // 16) ** -0.5, 0.75, ((0, 32),))
    b_out = noise(key_list[8], (D,), 0.2, 1.1953125, ((0, 32),))
    ln2_gain = jnp.clip(1.0 + 0.1 * jax.random.normal(key_list[9], (D,), jnp.float32), 0.5, 1.5).astype(jnp.bfloat16)
    ln2_shift = noise(key_list[10], (D,), 0.2, 1.1953125, ((0, 32),))
    w_fc1 = noise(key_list[11], (D, FF), D ** -0.5, 0.1875, ((0, 32),))
    b_fc1 = noise(key_list[12], (FF,), 0.2, 1.1953125, ((0, 32),))
    w_fc2 = noise(key_list[13], (FF, D), FF ** -0.5, 0.09375, ((0, 32),))
    b_fc2 = noise(key_list[14], (D,), 0.2, 1.1953125, ((0, 32),))
    return {"layer_in": layer_in, "grad_out": grad_out, "lengths": lengths, "ln1_gain": ln1_gain, "ln1_shift": ln1_shift, "w_qkv": w_qkv, "b_qv": b_qv, "w_out": w_out, "b_out": b_out, "ln2_gain": ln2_gain, "ln2_shift": ln2_shift, "w_fc1": w_fc1, "b_fc1": b_fc1, "w_fc2": w_fc2, "b_fc2": b_fc2}


EPS = 1e-05
HIGH = lax.Precision.HIGHEST

@jax.custom_vjp
def low(v):
    return lax.optimization_barrier(v.astype(jnp.bfloat16)).astype(jnp.float32)

@jax.custom_vjp
def low_back(v):
    return v

def low_keep(v):
    return (low(v), None)

def low_pass(kept, grad):
    return (grad,)

def back_keep(v):
    return (v, None)

def back_low(kept, grad):
    return (low(grad),)
low.defvjp(low_keep, low_pass)
low_back.defvjp(back_keep, back_low)

def norm_rows(values, gain_vec, shift_vec):
    average = lax.optimization_barrier(jnp.mean(values, axis=-1, keepdims=True))
    centred = values - average
    inv_std = lax.rsqrt(lax.optimization_barrier(jnp.mean(centred * centred, axis=-1, keepdims=True)) + EPS)
    return centred * inv_std * gain_vec + shift_vec

def gelu_tanh(values):
    return 0.5 * values * (1.0 + jnp.tanh(0.7978845608028654 * (values + 0.044715 * values * values * values)))

def head_slopes(count):
    return jnp.exp2(-8.0 * (jnp.arange(count, dtype=jnp.float32) + 1.0) / count)

def one_sequence(weights_all, seq_rows, seq_length):
    ln1_gain, ln1_shift, w_qkv, b_qv, w_out, b_out, ln2_gain, ln2_shift, w_fc1, b_fc1, w_fc2, b_fc2 = weights_all
    positions = jnp.arange(LEN, dtype=jnp.int32)
    live_rows = positions < seq_length
    normed = low(norm_rows(seq_rows, ln1_gain, ln1_shift))
    bias_full = jnp.concatenate([b_qv[:D], jnp.zeros((D,), seq_rows.dtype), b_qv[D:]])
    qkv = low(low_back(jnp.dot(normed, w_qkv, precision=HIGH) + bias_full))
    qkv = qkv.reshape(LEN, 3, HEADS, HD)
    queries = qkv[:, 0]
    keys_all = qkv[:, 1]
    values_all = qkv[:, 2]
    slopes = head_slopes(HEADS).astype(seq_rows.dtype)
    block_rows = min(512, LEN)

    def block_attend(offset):
        q_blk = lax.dynamic_slice_in_dim(queries, offset, block_rows, 0)
        scores = jnp.einsum('qhd,khd->hqk', q_blk, keys_all, precision=HIGH) * HD ** (-0.5)
        q_pos = offset + jnp.arange(block_rows, dtype=jnp.int32)
        gap_pos = (positions[None, :] - q_pos[:, None]).astype(seq_rows.dtype)
        scores = low_back(scores + slopes[:, None, None] * gap_pos[None])
        allowed = (positions[None, :] <= q_pos[:, None]) & live_rows[None, :]
        scores = jnp.where(allowed[None], scores, -1e+30)
        attn_probs = low(jax.nn.softmax(scores, axis=-1))
        return jnp.einsum('hqk,khd->qhd', attn_probs, values_all, precision=HIGH)
    offsets = (jnp.arange(LEN // block_rows, dtype=jnp.int32) * block_rows).astype(jnp.int32)
    head_out = lax.map(jax.checkpoint(block_attend), offsets).reshape(LEN, D)
    head_out = low(low_back(head_out))
    branch = low_back(jnp.dot(head_out, w_out, precision=HIGH) + b_out)
    middle = seq_rows + branch
    normed2 = low(norm_rows(middle, ln2_gain, ln2_shift))
    inner_act = low_back(jnp.dot(normed2, w_fc1, precision=HIGH) + b_fc1)
    activated = low(gelu_tanh(inner_act))
    mlp_out = low_back(jnp.dot(activated, w_fc2, precision=HIGH) + b_fc2)
    return jnp.where(live_rows[:, None], middle + mlp_out, 0.0)

def forward(weights_all, all_rows, lengths):
    seq_step = jax.checkpoint(one_sequence)

    def scan_step(running, item):
        return (running, seq_step(weights_all, item[0], item[1]))
    _, outputs = lax.scan(scan_step, 0.0, (all_rows, lengths))
    return outputs

def reference(layer_in, grad_out, lengths, ln1_gain, ln1_shift, w_qkv, b_qv, w_out, b_out, ln2_gain, ln2_shift, w_fc1, b_fc1, w_fc2, b_fc2):
    weights_all = tuple((item.astype(jnp.float32) for item in (ln1_gain, ln1_shift, w_qkv, b_qv, w_out, b_out, ln2_gain, ln2_shift, w_fc1, b_fc1, w_fc2, b_fc2)))
    all_rows = layer_in.astype(jnp.float32)
    outputs, pull_back = jax.vjp(lambda params, inputs: forward(params, inputs, lengths), weights_all, all_rows)
    grad_params, grad_rows = pull_back(grad_out.astype(jnp.float32))
    g_ln1g, g_ln1s, g_qkv, g_bqv, g_wout, g_bout, g_ln2g, g_ln2s, g_fc1, g_bfc1, g_fc2, g_bfc2 = grad_params
    return (outputs.astype(jnp.bfloat16), grad_rows.astype(jnp.bfloat16), g_ln1g, g_ln1s, g_qkv, g_bqv, g_wout, g_bout, g_ln2g, g_ln2s, g_fc1, g_bfc1, g_fc2, g_bfc2)
```

```python
import functools
import math

import jax
import jax.numpy as jnp
from jax import lax
from jax.experimental import pallas as pl
from jax.experimental.pallas import tpu as pltpu
from jax.sharding import PartitionSpec as P

HEADS = 16


EPS = 1e-05
LOG2E = 1.4426950408889634
f32 = jnp.float32
bf16 = jnp.bfloat16
MIB = 1024 * 1024

NN = (((1,), (0,)), ((), ()))
NT = (((1,), (1,)), ((), ()))
TN = (((0,), (0,)), ((), ()))


def mm(a, b, dims=NN):
    return lax.dot_general(a, b, dims, preferred_element_type=f32)


def norm_unit(values):
    average = jnp.mean(values, axis=-1, keepdims=True)
    centred = values - average
    inv_std = lax.rsqrt(jnp.mean(centred * centred, axis=-1, keepdims=True) + EPS)
    return centred * inv_std, inv_std


def norm_back(upstream, unit_rows, inv_std, gain_vec):
    scaled = upstream * gain_vec
    part_one = jnp.mean(scaled, axis=-1, keepdims=True)
    part_two = jnp.mean(scaled * unit_rows, axis=-1, keepdims=True)
    return inv_std * (scaled - part_one - unit_rows * part_two)


def colsum(values):
    return jnp.sum(values, axis=0, keepdims=True)


def whole(shape):
    return pl.BlockSpec(shape, lambda *_: (0,) * len(shape))


SMEM = pl.BlockSpec(memory_space=pltpu.SMEM)


def size_of(item):
    return math.prod(item.shape) * jnp.dtype(item.dtype).itemsize


def call(body, ins, in_specs, outs, scratch=(), room=6):
    blocks = [(item, spec) for item, spec in zip(ins, in_specs) if spec is not SMEM]
    need = 2 * sum(size_of(item) for item, _ in blocks) + 2 * sum(size_of(o) for o in outs)
    need += sum(size_of(item) for item in scratch)
    return pl.pallas_call(
        body,
        grid=(1,),
        in_specs=in_specs,
        out_specs=[whole(o.shape) for o in outs],
        out_shape=outs,
        scratch_shapes=list(scratch),
        compiler_params=pltpu.CompilerParams(
            vmem_limit_bytes=min(need + room * MIB, 60 * MIB)
        ),
        cost_estimate=pl.CostEstimate(flops=1, bytes_accessed=1, transcendentals=0),
    )(*ins)


def sds(shape, dtype):
    return jax.ShapeDtypeStruct(shape, dtype)


def fill_bias(bias_ref, slope, length):
    shape = bias_ref.shape
    pos = lax.broadcasted_iota(jnp.int32, shape, 0)
    bias_ref[...] = jnp.where(pos < length, pos.astype(f32) * (slope * LOG2E), -1e30)


def diag_mask(blk):
    key = lax.broadcasted_iota(jnp.int32, (blk, blk), 0)
    query = lax.broadcasted_iota(jnp.int32, (blk, blk), 1)
    return jnp.where(key <= query, 0.0, -1e30).astype(f32)


def lane_head(shape, head_dim, which):
    lane = lax.broadcasted_iota(jnp.int32, shape, 1)
    return (lane >= which * head_dim) & (lane < (which + 1) * head_dim)


def place_pieces(dst_ref, near, far, me_ref):
    piece = dst_ref.shape[0] // 32
    for b, blocks in enumerate((near, far)):
        for n in range(4):
            row = jnp.bitwise_xor(me_ref[1], 2 * n + b)
            for k in range(4):
                at = row * 4 + jnp.bitwise_xor(me_ref[2], k)
                dst_ref[pl.ds(pl.multiple_of(at * piece, piece), piece), :] = blocks[
                    n, k * piece : (k + 1) * piece, :
                ]


def place_spread(dst_ref, blocks, me_ref):
    piece = blocks[0].shape[1]
    for k, block in enumerate(blocks):
        for r in range(8):
            at = r * 4 + jnp.bitwise_xor(me_ref[2], k)
            dst_ref[pl.ds(pl.multiple_of(at * piece, piece), piece), :] = block[r]


def unpack_small(me_ref, near, far, cuts, par_ref):
    n_small = sum(cuts)
    pieces = jnp.concatenate(
        [item[:, -16:, :n_small].reshape(64, n_small) for item in (near, far)], axis=0
    )
    seq = me_ref[2]

    def owners(cols):
        p = lax.broadcasted_iota(jnp.int32, (128, cols), 0)
        lane = lax.broadcasted_iota(jnp.int32, (128, cols), 1)
        m = ((p >> 4) & 3) * 2 + (p >> 6)
        row = jnp.bitwise_xor(m, me_ref[1])
        member = jnp.bitwise_xor((p >> 2) & 3, seq)
        return row, member, lane, (p & 3) == 0

    def spread(at, size, cols):
        one = lax.broadcasted_iota(jnp.int32, (size, cols), 0)
        two = lax.broadcasted_iota(jnp.int32, (size, cols), 1) & (size - 1)
        table = jnp.where(one == two, 1.0, 0.0).astype(bf16)
        return mm(pieces[:, at : at + size], table)

    def pick(values, mask):
        return colsum(jnp.where(mask, values, 0.0))

    starts = [sum(cuts[:i]) for i in range(len(cuts))]
    width = par_ref.shape[1]
    row, member, lane, first = owners(width)
    size = cuts[0]
    mask = first & (row * 4 + member == lane >> (size.bit_length() - 1))
    for out, i in ((0, 0), (1, 1), (2, 3), (3, 4), (4, 5), (6, 7)):
        par_ref[out : out + 1, :] = pick(spread(starts[i], size, width), mask)
    size = cuts[6]
    mask = first & (member == seq) & (row == lane >> (size.bit_length() - 1))
    par_ref[5:6, :] = pick(spread(starts[6], size, width), mask)
    par_ref[7:8, :] = jnp.zeros((1, width), f32)
    size = cuts[2]
    gw = width // 4
    row, member, lane, first = owners(gw)
    mask = first & (member == lane >> (size.bit_length() - 1))
    values = spread(starts[2], size, gw)
    return jnp.concatenate(
        [
            pick(values, mask & (row == seq)),
            jnp.zeros((1, gw), f32),
            pick(values, mask & (row == seq + 4)),
        ],
        axis=1,
    )


def pick_kernel(me_ref, wq_ref, w1_ref, small_ref, q0, q1, q2, q3, f0, f1, f2, f3):
    gw = q0.shape[1] // 3
    width = 4 * gw
    fl = w1_ref.shape[1] // 32
    dl = wq_ref.shape[0]
    for k, (out_q, out_f) in enumerate(((q0, f0), (q1, f1), (q2, f2), (q3, f3))):
        group = jnp.bitwise_xor(me_ref[0], k)
        for t in range(3):
            at = pl.multiple_of(t * width + group * gw, gw)
            out_q[:dl, t * gw : (t + 1) * gw] = wq_ref[:, pl.ds(at, gw)]
        out_q[dl:, :] = jnp.broadcast_to(small_ref[...], (16, 3 * gw))
        for r in range(8):
            at = pl.multiple_of((r * 4 + group) * fl, fl)
            out_f[:, r * fl : (r + 1) * fl] = w1_ref[:, pl.ds(at, fl)]


def attend_kernel(
    me_ref, len_ref, slope_ref, x0, x1, x2, x3, w_near, w_far, par_in, bias_in,
    att_ref, qkv_ref, norm_ref, lse_ref, par_ref, bias_ref, att_t_ref, w_ref, *, cuts,
):
    if cuts:
        bias_row = unpack_small(me_ref, w_near, w_far, cuts, par_ref)
    else:
        par_ref[...] = par_in[...]
        bias_row = bias_in[...]
    place_pieces(w_ref, w_near, w_far, me_ref)
    blk = x0.shape[0]
    seq_len, gw3 = qkv_ref.shape
    gw = gw3 // 3
    heads_here = slope_ref.shape[0]
    hd = gw // heads_here
    scale = hd ** (-0.5) * LOG2E
    me = me_ref[0]
    for k, xk in enumerate((x0, x1, x2, x3)):
        at = pl.multiple_of(jnp.bitwise_xor(me, k) * blk, blk)
        unit, _ = norm_unit(xk[...].astype(f32))
        low = (unit * par_ref[0:1, :] + par_ref[1:2, :]).astype(bf16)
        norm_ref[pl.ds(at, blk), :] = low
        qkv_ref[pl.ds(at, blk), :] = (mm(low, w_ref[...]) + bias_row).astype(bf16)
    length = len_ref[0]
    mask = diag_mask(blk)
    lse_ref[...] = jnp.zeros(lse_ref.shape, f32)
    for pair in range(heads_here // 2):
        lanes = slice(pair * 2 * hd, (pair + 1) * 2 * hd)
        keys = qkv_ref[:, gw + pair * 2 * hd : gw + (pair + 1) * 2 * hd]
        vals_t = qkv_ref[:, 2 * gw + pair * 2 * hd : 2 * gw + (pair + 1) * 2 * hd].T
        for sub in range(2):
            head = pair * 2 + sub
            fill_bias(bias_ref, slope_ref[head], length)
            for i in range(seq_len // blk):
                q_rows = slice(i * blk, (i + 1) * blk)
                q_blk = qkv_ref[q_rows, lanes]
                q_blk = jnp.where(lane_head(q_blk.shape, hd, sub), q_blk, jnp.zeros((), bf16))
                span = (i + 1) * blk
                logits = mm(keys[:span], q_blk, NT) * scale + bias_ref[:span]
                edge = logits[i * blk :] + mask
                top = jnp.max(edge, axis=0, keepdims=True)
                if i:
                    top = jnp.maximum(top, jnp.max(logits[: i * blk], axis=0, keepdims=True))
                expo = jnp.exp2(edge - top)
                total = colsum(expo)
                vt = vals_t[sub * hd : (sub + 1) * hd]
                acc = mm(vt[:, i * blk : span], expo.astype(bf16))
                if i:
                    expo = jnp.exp2(logits[: i * blk] - top)
                    total = total + colsum(expo)
                    acc = acc + mm(vt[:, : i * blk], expo.astype(bf16))
                att_t_ref[head * hd : (head + 1) * hd, q_rows] = acc / total
                lse_ref[head : head + 1, q_rows] = top + jnp.log2(total)
    att_ref[...] = att_t_ref[...].T.astype(bf16)


def feed_kernel(
    me_ref, xa, xb, a0, a1, a2, a3, ga, gb, o0, o1, o2, o3,
    u_near, u_far, w2_ref, par_ref,
    *refs, flips,
):
    if flips[1]:
        odd_ref, norm_ref, act_ref, gin_ref, sum_ref, wo_ref, w1_ref = refs
        outs = (odd_ref.at[0], odd_ref.at[1])
    else:
        far_ref, own_ref, mid_ref, wh_ref, norm_ref, act_ref, gin_ref, sum_ref = refs[:8]
        wo_ref, w1_ref = refs[8:]
        outs = (far_ref, own_ref)
    blk = xa.shape[0]
    gw = a0.shape[1]
    place_spread(wo_ref, (o0, o1, o2, o3), me_ref)
    place_pieces(w1_ref, u_near, u_far, me_ref)
    w2 = w2_ref[...].reshape(w1_ref.shape)
    me = me_ref[0]
    if not flips[1]:
        wh_ref[...] = wo_ref[pl.ds(pl.multiple_of(me * gw, gw), gw), :]
    sums = jnp.zeros(sum_ref.shape, f32)
    for n, (flip, x_ref, g_ref) in enumerate(zip(flips, (xa, xb), (ga, gb))):
        at = pl.multiple_of(jnp.bitwise_xor(me, flip) * blk, blk)
        middle = x_ref[...].astype(f32) + par_ref[2:3, :]
        for kk, ak in enumerate((a0, a1, a2, a3)):
            w_at = pl.multiple_of(jnp.bitwise_xor(me, kk) * gw, gw)
            middle = middle + mm(ak[pl.ds(at, blk), :], wo_ref[pl.ds(w_at, gw), :])
        if flip == 0:
            mid_ref[...] = middle
        unit, _ = norm_unit(middle)
        low = (unit * par_ref[3:4, :] + par_ref[4:5, :]).astype(bf16)
        rows = slice(n * blk, (n + 1) * blk)
        norm_ref[rows, :] = low
        inner = mm(low, w1_ref[...]) + par_ref[5:6, :]
        grad_act = mm(g_ref[...], w2, NT)
        square = inner * inner
        th = jnp.tanh(0.7978845608028654 * (inner + 0.044715 * inner * square))
        half = 0.5 * (1.0 + th)
        act_ref[rows, :] = (inner * half).astype(bf16)
        slope = half + (0.5 * 0.7978845608028654) * inner * (1.0 - th * th) * (
            1.0 + 3.0 * 0.044715 * square
        )
        grad_inner = (grad_act * slope).astype(bf16)
        gin_ref[rows, :] = grad_inner
        sums = sums + colsum(grad_inner.astype(f32))
        part = mm(grad_inner, w1_ref[...], NT)
        outs[n][...] = part.astype(outs[n].dtype)
    sum_ref[...] = sums


def split_rows(me_ref, send_ref, keep_ref, product):
    size = send_ref.shape[1]
    for b, out in enumerate((keep_ref, send_ref)):
        for a in range(4):
            row = jnp.bitwise_xor(me_ref[1], 2 * a + b)
            out[a] = product(pl.multiple_of(row * size, size), size).astype(bf16)


def weight_one_kernel(me_ref, na_ref, nb_ref, ga_ref, gb_ref, send_ref, keep_ref):
    split_rows(
        me_ref,
        send_ref,
        keep_ref,
        lambda at, size: mm(na_ref[:, pl.ds(at, size)], ga_ref[...], TN)
        + mm(nb_ref[:, pl.ds(at, size)], gb_ref[...], TN),
    )


def weight_two_kernel(me_ref, aa_ref, ab_ref, g3, g1, g2, g0, send_ref, keep_ref):
    blk = g0.shape[0]

    def product(at, size):
        one = aa_ref[:, pl.ds(at, size)]
        two = ab_ref[:, pl.ds(at, size)]
        return (
            mm(one[:blk], g3[...], TN)
            + mm(one[blk:], g1[...], TN)
            + mm(two[:blk], g2[...], TN)
            + mm(two[blk:], g0[...], TN)
        )

    split_rows(me_ref, send_ref, keep_ref, product)


def weight_qkv_kernel(me_ref, lhs_ref, rhs_ref, send_ref, keep_ref):
    split_rows(
        me_ref,
        send_ref,
        keep_ref,
        lambda at, size: mm(lhs_ref[:, pl.ds(at, size)], rhs_ref[...], TN),
    )


def out_weight_kernel(
    me_ref, a0, a1, a2, a3, b0, b1, b2, b3, send_ref, keep_ref, gb_ref, all_ref
):
    blk = b0.shape[0]
    gw = a0.shape[1]
    dl = send_ref.shape[1]
    for k, bk in enumerate((b0, b1, b2, b3)):
        at = pl.multiple_of(jnp.bitwise_xor(me_ref[0], k) * blk, blk)
        gb_ref[pl.ds(at, blk), :] = bk[...]
    for kk, ak in enumerate((a0, a1, a2, a3)):
        w_at = pl.multiple_of(jnp.bitwise_xor(me_ref[0], kk) * gw, gw)
        all_ref[pl.ds(w_at, gw), :] = mm(ak[...], gb_ref[...], TN)
    for b, out in enumerate((keep_ref, send_ref)):
        for a in range(4):
            at = (jnp.bitwise_xor(me_ref[1], 2 * a + b) * 4 + me_ref[0]) * dl
            out[a] = all_ref[pl.ds(pl.multiple_of(at, dl), dl), :].astype(bf16)


def add_half_kernel(keep_ref, got_ref, send_ref, left_ref):
    for n, a in enumerate((1, 3)):
        send_ref[n] = (keep_ref[a].astype(f32) + got_ref[a].astype(f32)).astype(bf16)
    for n, a in enumerate((0, 2)):
        left_ref[n] = keep_ref[a].astype(f32) + got_ref[a].astype(f32)


def add_last_kernel(left_ref, got_ref, send_ref, last_ref):
    send_ref[...] = (left_ref[1] + got_ref[1].astype(f32)).astype(bf16)
    last_ref[...] = left_ref[0] + got_ref[0].astype(f32)


def add_all_kernel(me_ref, keep_ref, got_ref, out_ref):
    for a in range(4):
        z = jnp.bitwise_xor(lax.shift_right_logical(me_ref[1], 1), a)
        out_ref[z] = (keep_ref[a].astype(f32) + got_ref[a].astype(f32)).astype(bf16)


def sum_kernel(in_ref, out_ref):
    total = in_ref[0].astype(f32)
    for n in range(1, in_ref.shape[0]):
        total = total + in_ref[n].astype(f32)
    out_ref[...] = total


def total_kernel(last_ref, *refs):
    total = last_ref[...]
    for got in refs[:-1]:
        total = total + got[...].astype(f32)
    refs[-1][...] = total


def cut_parts(me_ref, all_ref, outs):
    dl = outs[0].shape[0]
    for k, out in enumerate(outs):
        at = pl.multiple_of(jnp.bitwise_xor(me_ref[0], k) * dl, dl)
        out[...] = all_ref[pl.ds(at, dl), :].astype(out.dtype)


def parts_kernel(me_ref, last_ref, got_ref, qkv_ref, o0, o1, o2, o3, all_ref):
    width = last_ref.shape[1]
    all_ref[:, :width] = last_ref[...] + got_ref[...].astype(f32)
    total = qkv_ref[0].astype(f32)
    for n in range(1, qkv_ref.shape[0]):
        total = total + qkv_ref[n].astype(f32)
    all_ref[:, width:] = total
    cut_parts(me_ref, all_ref, (o0, o1, o2, o3))


def spread_both_kernel(me_ref, i0, i1, i2, i3, one_ref, qkv_ref):
    pieces = (i0, i1, i2, i3)
    width = one_ref.shape[1] // 4
    for out_ref, base, size in ((one_ref, 0, width // 8), (qkv_ref, width, width // 4)):
        for k, piece in enumerate(pieces):
            for t in range(out_ref.shape[1] // (4 * size)):
                at = (t * 4 + jnp.bitwise_xor(me_ref[0], k)) * size
                out_ref[:, pl.ds(pl.multiple_of(at, size), size)] = piece[
                    :, base + t * size : base + (t + 1) * size
                ].astype(f32)


def pack_small_kernel(me_ref, one_ref, two_ref, ba_ref, bb_ref, col_ref, out_ref, *, cuts):
    count = out_ref.shape[0]
    width = one_ref.shape[1]
    gw = width // 4

    def fold(values, size, owner, cols):
        lane = lax.broadcasted_iota(jnp.int32, (count, cols), 1)
        device = lax.broadcasted_iota(jnp.int32, (count, cols), 0)
        mine = jnp.where(owner(lane >> (size.bit_length() - 1), device), values, 0.0)
        one = lax.broadcasted_iota(jnp.int32, (cols, size), 0) & (size - 1)
        two = lax.broadcasted_iota(jnp.int32, (cols, size), 1)
        table = jnp.where(one == two, 1.0, 0.0).astype(f32)
        return lax.dot_general(
            mine, table, NN, precision=lax.Precision.HIGHEST, preferred_element_type=f32
        )

    def plain(values):
        return fold(values, cuts[0], lambda part, device: part == device, width)

    member = me_ref[0]
    query = fold(col_ref[:, :gw], cuts[2], lambda p, d: p + 4 * member == d, gw)
    value = fold(col_ref[:, 2 * gw :], cuts[2], lambda p, d: p + 4 * member + 16 == d, gw)
    hidden = fold(ba_ref[...] + bb_ref[...], cuts[6], lambda p, d: p * 4 + member == d, width)
    out_ref[...] = jnp.concatenate(
        [
            plain(one_ref[0:1, :]),
            plain(one_ref[1:2, :]),
            query + value,
            plain(two_ref[2:3, :]),
            plain(two_ref[0:1, :]),
            plain(two_ref[1:2, :]),
            hidden,
            plain(two_ref[3:4, :]),
        ],
        axis=1,
    )


def mlp_kernel(aa_ref, ab_ref, w2_ref, odd_ref, far_ref, own_ref):
    blk = own_ref.shape[0]
    w2 = w2_ref[...].reshape(aa_ref.shape[1], own_ref.shape[1])
    odd_ref[0] = mm(aa_ref[:blk], w2).astype(bf16)
    odd_ref[1] = mm(aa_ref[blk:], w2).astype(bf16)
    far_ref[...] = mm(ab_ref[:blk], w2)
    own_ref[...] = mm(ab_ref[blk:], w2)


def middle_kernel(own, near, far, mid_ref, g0, par_ref, gb_ref, gm_ref, sum_ref):
    upstream = own[...] + near[1].astype(f32) + far[...].astype(f32)
    unit, inv = norm_unit(mid_ref[...])
    grad_mlp = g0[...].astype(f32)
    grad_middle = grad_mlp + norm_back(upstream, unit, inv, par_ref[3:4, :])
    low = grad_middle.astype(bf16)
    gm_ref[...] = grad_middle
    gb_ref[...] = low
    sum_ref[0:1, :] = colsum(upstream * unit)
    sum_ref[1:2, :] = colsum(upstream)
    sum_ref[2:3, :] = colsum(low.astype(f32))
    sum_ref[3:4, :] = colsum(grad_mlp)


def back_kernel(
    me_ref, len_ref, slope_ref, b0, b1, b2, b3, wh_ref, qkv_ref, lse_ref,
    dqkv_ref, ga_ref, bias_ref, dk_ref, dv_ref, dqt_ref,
):
    blk = b0.shape[0]
    seq_len, gw3 = qkv_ref.shape
    gw = gw3 // 3
    heads_here = slope_ref.shape[0]
    hd = gw // heads_here
    scale = hd ** (-0.5)
    me = me_ref[0]
    w_heads = wh_ref[...]
    for k, bk in enumerate((b0, b1, b2, b3)):
        at = pl.multiple_of(jnp.bitwise_xor(me, k) * blk, blk)
        ga_ref[pl.ds(at, blk), :] = mm(bk[...], w_heads, NT).astype(bf16)
    length = len_ref[0]
    mask = diag_mask(blk)
    none = jnp.zeros((), bf16)
    for pair in range(heads_here // 2):
        lanes = slice(pair * 2 * hd, (pair + 1) * 2 * hd)
        k_lanes = slice(gw + pair * 2 * hd, gw + (pair + 1) * 2 * hd)
        v_lanes = slice(2 * gw + pair * 2 * hd, 2 * gw + (pair + 1) * 2 * hd)
        keys = qkv_ref[:, k_lanes]
        keys_t = keys.T
        vals = qkv_ref[:, v_lanes]
        dk_ref[...] = jnp.zeros(dk_ref.shape, f32)
        dv_ref[...] = jnp.zeros(dv_ref.shape, f32)
        for sub in range(2):
            head = pair * 2 + sub
            fill_bias(bias_ref, slope_ref[head], length)
            for i in range(seq_len // blk):
                q_rows = slice(i * blk, (i + 1) * blk)
                span = (i + 1) * blk
                pick = lane_head((blk, 2 * hd), hd, sub)
                q_blk = jnp.where(pick, qkv_ref[q_rows, lanes], none)
                g_blk = jnp.where(pick, ga_ref[q_rows, lanes], none)
                logits = mm(keys[:span], q_blk, NT) * (scale * LOG2E) + bias_ref[:span]
                lse = lse_ref[head : head + 1, q_rows]
                edge = jnp.exp2(logits[i * blk :] + mask - lse)
                if i:
                    soft = jnp.concatenate([jnp.exp2(logits[: i * blk] - lse), edge], axis=0)
                else:
                    soft = edge
                grad_soft = mm(vals[:span], g_blk, NT)
                row_dot = colsum(soft * grad_soft)
                grad_scores = (soft * (grad_soft - row_dot)).astype(bf16)
                soft_low = soft.astype(bf16)
                dv_ref[:span] += mm(soft_low, g_blk)
                dk_ref[:span] += mm(grad_scores, q_blk)
                dqt_ref[sub * hd : (sub + 1) * hd, q_rows] = mm(
                    keys_t[sub * hd : (sub + 1) * hd, :span], grad_scores
                )
        dqkv_ref[:, lanes] = (dqt_ref[...].T * scale).astype(bf16)
        dqkv_ref[:, k_lanes] = (dk_ref[...] * scale).astype(bf16)
        dqkv_ref[:, v_lanes] = dv_ref[...].astype(bf16)


def first_norm_kernel(
    me_ref, x0, x1, x2, x3, dqkv_ref, w_near, w_far,
    odd_ref, far_ref, own_ref, sum_ref, col_ref, w_ref,
):
    blk = x0.shape[0]
    place_pieces(w_ref, w_near, w_far, me_ref)
    me = me_ref[0]
    gain = jnp.zeros((1, x0.shape[1]), f32)
    shift = gain
    cols = jnp.zeros(col_ref.shape, f32)
    for k in (3, 2, 1, 0):
        xk = (x0, x1, x2, x3)[k]
        out = (own_ref, odd_ref.at[1], far_ref, odd_ref.at[0])[k]
        at = pl.multiple_of(jnp.bitwise_xor(me, k) * blk, blk)
        grad = dqkv_ref[pl.ds(at, blk), :]
        part = mm(grad, w_ref[...], NT)
        out[...] = part.astype(out.dtype)
        unit, _ = norm_unit(xk[...].astype(f32))
        gain = gain + colsum(part * unit)
        shift = shift + colsum(part)
        cols = cols + colsum(grad.astype(f32))
    sum_ref[0:1, :] = gain
    sum_ref[1:2, :] = shift
    col_ref[...] = cols


def input_kernel(own, near, far, x_ref, gm_ref, par_ref, out_ref):
    upstream = own[...] + near[1].astype(f32) + far[...].astype(f32)
    unit, inv = norm_unit(x_ref[...].astype(f32))
    out_ref[...] = (gm_ref[...] + norm_back(upstream, unit, inv, par_ref[0:1, :])).astype(bf16)


def head_slopes(count):
    return jnp.exp2(-8.0 * (jnp.arange(count, dtype=f32) + 1.0) / count)


def per_device(
    layer_in,
    grad_out,
    lengths,
    ln1_gain,
    ln1_shift,
    w_qkv,
    b_qv,
    w_out,
    b_out,
    ln2_gain,
    ln2_shift,
    w_fc1,
    b_fc1,
    w_fc2,
    b_fc2,
):
    rows = lax.axis_size("rows")
    groups = lax.axis_size("seq")
    everyone = rows * groups
    my_group = lax.axis_index("seq")
    my_row = lax.axis_index("rows")
    blk = layer_in.shape[1]
    width = layer_in.shape[2]
    seq_len = blk * groups
    heads_here = HEADS // groups
    gw = width // groups
    dl = w_qkv.shape[0]
    fl = w_fc2.shape[0]
    hidden = rows * fl
    cut = width // 8
    assert groups == 4 and hidden == width
    direct = rows == 8
    me = jnp.stack([my_group, my_row, my_group]).astype(jnp.int32)
    if not direct:
        me = me * jnp.array([1, 0, 0], jnp.int32)

    def swap(values, flip):
        return lax.ppermute(values, "seq", [(i, i ^ flip) for i in range(groups)])

    def swap_x(values):
        return lax.ppermute(values, "rows", [(i, i ^ 1) for i in range(rows)])

    def swap_z(values, flip):
        return lax.ppermute(values, "rows", [(i, i ^ (2 * flip)) for i in range(rows)])

    def exchange_z(values):
        return lax.all_to_all(
            values,
            "rows",
            split_axis=0,
            concat_axis=0,
            axis_index_groups=[[2 * z + x for z in range(rows // 2)] for x in range(2)],
            tiled=True,
        )

    def gather_z(values):
        return [values] + [swap_z(values, a) for a in (1, 2, 3)]

    def after(values, *others):
        return lax.optimization_barrier((values, *others))[0]

    def gather_seq(values):
        far = swap(values, 2)
        return [values, swap(values, 1), far, swap(far, 1)]

    def far_sum(far, near):
        return (far + near[0].astype(f32)).astype(bf16)

    parts = [ln1_gain, ln1_shift, b_qv, b_out, ln2_gain, ln2_shift, b_fc1, b_fc2]
    cuts = tuple(part.shape[0] for part in parts)
    n_small = sum(cuts)
    small = jnp.zeros((1, 3 * gw), bf16)
    at = 0
    for part in parts:
        n = part.shape[0]
        small = small + jnp.pad(part.reshape(1, n), ((0, 0), (at, 3 * gw - at - n)))
        at += n

    if direct:
        w2_all = jnp.concatenate([w_fc2, w_out], axis=0)
        w2_all = lax.all_gather(w2_all, "rows", axis=0, tiled=False)
        picked = call(
            pick_kernel,
            (me, w_qkv, w_fc1, small),
            [SMEM, whole(w_qkv.shape), whole(w_fc1.shape), whole(small.shape)],
            [sds((dl + 16, 3 * gw), bf16)] * 4 + [sds((dl, hidden), bf16)] * 4,
        )
        got = [picked[0]] + [swap(picked[k], k) for k in (1, 2, 3)]
        wq_block = jnp.concatenate(
            [item[:dl] for item in got] + [item[dl : dl + 4] for item in got], axis=0
        )
        wq_z = gather_z(wq_block)
        picked_late = [after(item, wq_block) for item in picked[4:]]
        w1_block = jnp.concatenate(
            [picked_late[0]] + [swap(picked_late[k], k) for k in (1, 2, 3)], axis=0
        )
        x_own = after(layer_in[0], w1_block)
    else:
        wq_parts = w_qkv.reshape(dl, 3, groups, gw).transpose(2, 0, 1, 3)
        f1_parts = w_fc1.reshape(dl, rows, groups, fl).transpose(2, 0, 1, 3)
        stage = jnp.concatenate(
            [f1_parts.reshape(groups, dl, hidden), wq_parts.reshape(groups, dl, 3 * gw)], axis=2
        )
        stage = lax.all_to_all(stage, "seq", split_axis=0, concat_axis=0, tiled=True)
        stage = lax.all_gather(
            stage.reshape(groups * dl, hidden + 3 * gw), "rows", axis=0, tiled=True
        )
        stage = stage.reshape(4, 2, cut, hidden + 3 * gw)
        w1_near, w1_far = stage[:, 0, :, :hidden], stage[:, 1, :, :hidden]
        wq_near, wq_far = stage[:, 0, :, hidden:], stage[:, 1, :, hidden:]
        w2_all = lax.all_gather(w_fc2, "rows", axis=0, tiled=True).reshape(8, cut, width)
        wo_mine = lax.all_gather(w_out, "rows", axis=0, tiled=False)
        wo_mine = wo_mine.reshape(8, width // 32, width)
        x_own = layer_in[0]
    par = jnp.zeros((8, width), f32)
    bias_mine = jnp.zeros((1, 3 * gw), f32)
    if not direct:
        full = lax.all_gather(small[:, :n_small], ("rows", "seq"), axis=0, tiled=True).astype(f32)
        ends = [sum(cuts[: i + 1]) for i in range(len(cuts))]
        full = [full[:, e - n : e].reshape(1, -1) for e, n in zip(ends, cuts)]
        bqv = lax.dynamic_index_in_dim(
            full[2].reshape(2, groups, gw), my_group, 1, keepdims=False
        )
        bias_mine = jnp.concatenate([bqv[0:1], jnp.zeros((1, gw), f32), bqv[1:2]], axis=1)
        bfc1 = lax.dynamic_index_in_dim(
            full[6].reshape(rows, groups, fl), my_group, 1, keepdims=False
        ).reshape(1, hidden)
        par = jnp.concatenate(
            [full[0], full[1], full[3], full[4], full[5], bfc1, full[7], full[7]], axis=0
        )

    positions = my_group * blk + jnp.arange(blk, dtype=jnp.int32)
    live_own = (positions < lengths[0])[:, None]
    x_far = swap(x_own, 2)
    x_near = swap(x_own, 1)
    g_own = jnp.where(live_own, grad_out[0], jnp.zeros((), bf16))
    if direct:
        wq_near = after(jnp.stack(wq_z), x_near, x_far)
        wq_far = swap_x(wq_near)
        x_far = after(x_far, wq_near)
        w1_z = gather_z(after(w1_block, wq_near))
        g_own = after(g_own, wq_near)
    g_far = swap(g_own, 2)
    xs = [x_own, x_near, x_far, swap(x_far, 1)]
    slopes = lax.dynamic_slice_in_dim(head_slopes(HEADS), my_group * heads_here, heads_here)

    x_spec = whole((blk, width))
    odd_spec = whole((2, blk, width))
    a_spec = whole((seq_len, gw))
    par_spec = whole((8, width))
    wq_spec = whole(wq_near.shape)
    w_spec = whole((4, cut, width))
    w2_spec = pl.BlockSpec((8, cut, width), lambda *_: (0, 0, 0))
    wo_spec = whole((8, width // 32, width))
    qkv_spec = whole((seq_len, 3 * gw))
    act_shape = (seq_len, width)
    half_shape = (2 * blk, width)

    att, qkv, normed, lse, par = call(
        functools.partial(attend_kernel, cuts=cuts if direct else ()),
        (me, lengths, slopes, *xs, wq_near, wq_far, par, bias_mine),
        [SMEM] * 3 + [x_spec] * 4 + [wq_spec] * 2 + [par_spec, whole((1, 3 * gw))],
        [
            sds((seq_len, gw), bf16),
            sds((seq_len, 3 * gw), bf16),
            sds(act_shape, bf16),
            sds((8, seq_len), f32),
            sds((8, width), f32),
        ],
        [
            pltpu.VMEM((seq_len, blk), f32),
            pltpu.VMEM((gw, seq_len), f32),
            pltpu.VMEM((width, 3 * gw), bf16),
        ],
    )
    atts = gather_seq(att)
    if direct:
        w1_near = jnp.stack([after(item, att) for item in w1_z])
        w1_far = swap_x(w1_near)
        wo_mine = after(w2_all, att)[:, cut:]
    wos = gather_seq(wo_mine)
    g_near, g_far = after(g_own, att), after(g_far, att)
    gs = [g_own, swap(g_near, 1), g_far, swap(g_far, 1)]
    if not direct:
        wo_all = jnp.stack(wos)[jnp.arange(4, dtype=jnp.int32) ^ my_group]
        wo_all = wo_all.reshape(4, rows, dl, width).transpose(1, 0, 2, 3)
        wo_all = wo_all.reshape(8, 4, width // 32, width)
        wos = [wo_all[:, k] for k in range(4)]


    def feed(flips, outs):
        return call(
            functools.partial(feed_kernel, flips=flips),
            (
                me, *(xs[k] for k in flips), *atts, *(gs[k] for k in flips), *wos, w1_near, w1_far,
                w2_all, par,
            ),
            [SMEM] + [x_spec] * 2 + [a_spec] * 4 + [x_spec] * 2 + [wo_spec] * 4 + [w_spec] * 2
            + [w2_spec, par_spec],
            outs + [sds(half_shape, bf16)] * 3 + [sds((1, width), f32)],
            [pltpu.VMEM((width, width), bf16)] * 2,
        )

    odd_list = [sds((2, blk, width), bf16)]
    even_list = [sds((blk, width), f32)] * 2
    odd, norm_a, act_a, gin_a, bsum_a = feed((3, 1), odd_list)
    near = swap(odd, 1)
    xs = [after(item, odd) for item in xs]
    far, own, middle, w_heads, norm_b, act_b, gin_b, bsum_b = feed(
        (2, 0), even_list + [sds((blk, width), f32), sds((gw, width), bf16)]
    )
    far = far_sum(far, near)
    act_b = after(act_b, far)
    far = swap(far, 2)
    half_spec = whole(half_shape)
    split_list = [sds((4, cut, width), bf16)] * 2
    one_send, one_keep = call(
        weight_one_kernel,
        (me, after(norm_a, act_b), norm_b, gin_a, gin_b),
        [SMEM] + [half_spec] * 4,
        split_list,
    )
    two_send, two_keep = call(
        weight_two_kernel,
        (me, act_a, after(act_b, one_keep), gs[3], gs[1], gs[2], gs[0]),
        [SMEM] + [half_spec] * 2 + [x_spec] * 4,
        split_list,
    )
    gb, grad_middle, sums_two = call(
        middle_kernel,
        (after(own, two_keep), near, far, middle, gs[0], par),
        [x_spec, odd_spec] + [x_spec] * 3 + [par_spec],
        [sds((blk, width), bf16), sds((blk, width), f32), sds((4, width), f32)],
    )
    m_odd, m_far, m_own = call(
        mlp_kernel,
        (after(act_a, gb), act_b, w2_all),
        [half_spec] * 2 + [w2_spec],
        odd_list + even_list,
    )
    gb_far = after(swap(gb, 2), m_own)
    gbs = [gb, swap(gb, 1), gb_far, swap(gb_far, 1)]

    def add_half(send, keep, late):
        size, cols = keep.shape[1:]
        return call(
            add_half_kernel,
            (after(keep, late), swap_x(send)),
            [whole(keep.shape)] * 2,
            [sds((2, size, cols), bf16), sds((2, size, cols), f32)],
        )

    def add_last(halves, late):
        send, left = halves
        size, cols = left.shape[1:]
        return call(
            add_last_kernel,
            (after(left, late), swap_z(send, 1)),
            [whole(left.shape)] * 2,
            [sds((size, cols), bf16), sds((size, cols), f32)],
        )

    def add_all(send, keep, late):
        return call(
            add_all_kernel,
            (me, after(keep, late), swap_x(send)),
            [SMEM] + [whole(keep.shape)] * 2,
            [sds(keep.shape, bf16)],
        )[0]

    def sum_z(values, late):
        size, cols = values.shape[1:]
        return call(
            sum_kernel,
            (after(values, late),),
            [whole(values.shape)],
            [sds((size, cols), f32)],
        )[0]

    def total(ins, late):
        spec = whole(ins[0].shape)
        return call(
            total_kernel,
            (after(ins[0], late), *ins[1:]),
            [spec] * len(ins),
            [sds(ins[0].shape, f32)],
        )[0]

    late = m_own
    if direct:
        one_half = add_half(one_send, one_keep, gbs[2])
        late = one_half[1]
    (dqkv,) = call(
        back_kernel,
        (me, lengths, slopes, after(gbs[0], late), *gbs[1:], w_heads, qkv, lse),
        [SMEM] * 3 + [x_spec] * 5 + [qkv_spec, whole((8, seq_len))],
        [sds((seq_len, 3 * gw), bf16)],
        [
            pltpu.VMEM((seq_len, gw), bf16),
            pltpu.VMEM((seq_len, blk), f32),
            pltpu.VMEM((seq_len, gw // 2), f32),
            pltpu.VMEM((seq_len, gw // 2), f32),
            pltpu.VMEM((gw // 2, seq_len), f32),
        ],
    )
    n_odd, n_far, n_own, sums_one, cols = call(
        first_norm_kernel,
        (me, *xs, dqkv, wq_near, wq_far),
        [SMEM] + [x_spec] * 4 + [qkv_spec] + [wq_spec] * 2,
        odd_list + even_list + [sds((2, width), f32), sds((1, 3 * gw), f32)],
        [pltpu.VMEM((width, 3 * gw), bf16)],
    )
    n_near = swap(n_odd, 1)
    late = n_own
    if direct:
        one_last = add_last(one_half, late)
        late = one_last[1]
    dq_send, dq_keep = call(
        weight_qkv_kernel,
        (me, normed, after(dqkv, late)),
        [SMEM, whole(act_shape), qkv_spec],
        [sds((4, cut, 3 * gw), bf16)] * 2,
    )
    if direct:
        two_half = add_half(two_send, two_keep, dq_keep)
        qkv_all = add_all(dq_send, dq_keep, two_half[1])
        late = qkv_all
        qkv_all = exchange_z(qkv_all)
    n_far = far_sum(after(n_far, late), n_near)
    late = n_far
    n_far = swap(n_far, 2)
    if direct:
        one_got = swap_z(one_last[0], 2)
    m_near = swap(m_odd, 1)

    def parts_of(values):
        cols = values.shape[-1]
        total = jnp.sum(values.reshape(rows, 4, dl, cols).astype(f32), axis=0).astype(bf16)
        return [
            lax.dynamic_index_in_dim(total, my_group ^ k, 0, keepdims=False) for k in range(4)
        ]

    def spread(pieces, parts):
        pieces = [pieces[0]] + [swap(pieces[k], k) for k in (1, 2, 3)]
        size = pieces[0].shape[1] // parts
        order = jnp.arange(4, dtype=jnp.int32) ^ my_group
        stacked = jnp.stack(pieces)[order].reshape(4, dl, parts, size)
        return stacked.transpose(1, 2, 0, 3).reshape(dl, 4 * parts * size).astype(f32)

    if direct:
        (small_grads,) = call(
            functools.partial(pack_small_kernel, cuts=cuts),
            (me, after(sums_one, late), sums_two, bsum_a, bsum_b, cols),
            [SMEM]
            + [whole(item.shape) for item in (sums_one, sums_two, bsum_a, bsum_b, cols)],
            [sds((everyone, n_small), f32)],
        )
    else:
        mine = (jnp.arange(groups) == my_group).astype(f32)
        bqv_sums = jnp.concatenate([cols[:, :gw], cols[:, 2 * gw :]], axis=0)
        grad_bqv = mine[None, :, None] * bqv_sums[:, None, :]
        grad_bfc1 = mine[None, :, None] * (bsum_a + bsum_b).reshape(rows, 1, fl)
        small_grads = jnp.concatenate(
            [
                part.reshape(everyone, -1)
                for part in (
                    sums_one[0],
                    sums_one[1],
                    grad_bqv,
                    sums_two[2],
                    sums_two[0],
                    sums_two[1],
                    grad_bfc1,
                    sums_two[3],
                )
            ],
            axis=1,
        )
    late = small_grads
    if direct:
        out_send, out_keep = call(
            out_weight_kernel,
            (me, *atts, after(gbs[0], late), *gbs[1:]),
            [SMEM] + [a_spec] * 4 + [x_spec] * 4,
            [sds((4, dl, width), bf16)] * 2,
            [pltpu.VMEM((seq_len, width), bf16), pltpu.VMEM((width, width), f32)],
        )
        two_last = add_last(two_half, out_keep)
        late = two_last[1]
    m_far = far_sum(after(m_far, late), m_near)
    late = m_far
    m_far = swap(m_far, 2)
    if direct:
        spec = whole((cut, width))
        pieces = call(
            parts_kernel,
            (me, after(one_last[1], late), one_got, qkv_all),
            [SMEM, spec, spec, whole(qkv_all.shape)],
            [sds((dl, width + 3 * gw), bf16)] * 4,
            [pltpu.VMEM((cut, width + 3 * gw), f32)],
        )
        small_grads = after(small_grads, pieces[0])
        out_all = add_all(out_send, out_keep, pieces[0])
        s_wfc2 = total((two_last[1], swap_z(two_last[0], 2)), out_all)
        late = s_wfc2
    small_grads = lax.all_to_all(
        small_grads, ("rows", "seq"), split_axis=0, concat_axis=0, tiled=True
    )
    if direct:
        n_own = after(n_own, small_grads)
    (grad_input,) = call(
        input_kernel,
        (after(n_own, late), n_near, n_far, layer_in[0], grad_middle, par),
        [x_spec, odd_spec] + [x_spec] * 3 + [par_spec],
        [sds((blk, width), bf16)],
    )
    if not direct:

        def rows_sum(send, keep):
            both = jnp.stack([keep, send], axis=1).reshape(rows, -1, keep.shape[-1])
            return lax.all_to_all(both, "rows", split_axis=0, concat_axis=0, tiled=True)

        one_parts = parts_of(rows_sum(one_send, one_keep))
        qkv_parts = parts_of(rows_sum(dq_send, dq_keep))
        s_wfc2 = jnp.sum(rows_sum(two_send, two_keep).astype(f32), axis=0)
        order = jnp.arange(4, dtype=jnp.int32) ^ my_group
        att_full = jnp.stack(atts)[order].transpose(1, 0, 2).reshape(seq_len, width)
        gb_full = jnp.stack(gbs)[order].reshape(seq_len, width)
        dw_out = mm(att_full, gb_full, TN).astype(bf16).reshape(rows, groups, dl, width)
        dw_out = lax.dynamic_index_in_dim(dw_out, my_group, 1, keepdims=False)
        got_out = lax.all_to_all(dw_out, "rows", split_axis=0, concat_axis=0, tiled=True)
        s_wout = jnp.sum(got_out.astype(f32), axis=0)
    if direct:
        pieces = [after(pieces[0], grad_input)] + [swap(pieces[k], k) for k in (1, 2, 3)]
        s_wfc1, s_wqkv = call(
            spread_both_kernel,
            (me, *pieces),
            [SMEM] + [whole(pieces[0].shape)] * 4,
            [sds((dl, 4 * width), f32), sds((dl, 3 * width), f32)],
        )
        s_wout = sum_z(exchange_z(out_all), s_wqkv)
    else:
        s_wfc1 = spread(one_parts, rows)
        s_wqkv = spread(qkv_parts, 3)

    mlp_own = m_own + m_near[1].astype(f32) + m_far.astype(f32)
    layer_result = jnp.where(live_own, middle + mlp_own + par[6:7], 0.0).astype(bf16)

    s_small = jnp.sum(small_grads, axis=0)
    smalls = []
    at = 0
    for n in cuts:
        smalls.append(s_small[at : at + n])
        at += n
    (s_gain_one, s_shift_one, s_bqv, s_bout, s_gain_two, s_shift_two, s_bfc1, s_bfc2) = smalls
    return (
        layer_result[None],
        grad_input[None],
        s_gain_one,
        s_shift_one,
        s_wqkv,
        s_bqv,
        s_wout,
        s_bout,
        s_gain_two,
        s_shift_two,
        s_wfc1,
        s_bfc1,
        s_wfc2,
        s_bfc2,
    )


def solution(mesh):
    both = P(("rows", "seq"))
    wide = P(("rows", "seq"), None)
    acts = P("rows", "seq", None)
    in_specs = (
        acts,
        acts,
        P("rows"),
        both,
        both,
        wide,
        both,
        wide,
        both,
        both,
        both,
        wide,
        both,
        wide,
        both,
    )
    out_specs = (
        acts,
        acts,
        both,
        both,
        wide,
        both,
        wide,
        both,
        both,
        both,
        wide,
        both,
        wide,
        both,
    )
    return jax.shard_map(
        per_device, mesh=mesh, in_specs=in_specs, out_specs=out_specs, check_vma=False
    )
```

```python
import functools
import math

import jax
import jax.numpy as jnp
from jax import lax
from jax.experimental import pallas as pl
from jax.experimental.pallas import tpu as pltpu
from jax.sharding import PartitionSpec as P

HEADS = 16


EPS = 1e-05
LOG2E = 1.4426950408889634
f32 = jnp.float32
bf16 = jnp.bfloat16
MIB = 1024 * 1024

NN = (((1,), (0,)), ((), ()))
NT = (((1,), (1,)), ((), ()))
TN = (((0,), (0,)), ((), ()))


def mm(a, b, dims=NN):
    return lax.dot_general(a, b, dims, preferred_element_type=f32)


def norm_unit(values):
    average = jnp.mean(values, axis=-1, keepdims=True)
    centred = values - average
    inv_std = lax.rsqrt(jnp.mean(centred * centred, axis=-1, keepdims=True) + EPS)
    return centred * inv_std, inv_std


def norm_back(upstream, unit_rows, inv_std, gain_vec):
    scaled = upstream * gain_vec
    part_one = jnp.mean(scaled, axis=-1, keepdims=True)
    part_two = jnp.mean(scaled * unit_rows, axis=-1, keepdims=True)
    return inv_std * (scaled - part_one - unit_rows * part_two)


def colsum(values):
    return jnp.sum(values, axis=0, keepdims=True)


def whole(shape):
    return pl.BlockSpec(shape, lambda *_: (0,) * len(shape))


SMEM = pl.BlockSpec(memory_space=pltpu.SMEM)


def size_of(item):
    return math.prod(item.shape) * jnp.dtype(item.dtype).itemsize


def call(body, ins, in_specs, outs, scratch=(), room=6):
    blocks = [(item, spec) for item, spec in zip(ins, in_specs) if spec is not SMEM]
    need = 2 * sum(size_of(item) for item, _ in blocks) + 2 * sum(size_of(o) for o in outs)
    need += sum(size_of(item) for item in scratch)
    return pl.pallas_call(
        body,
        grid=(1,),
        in_specs=in_specs,
        out_specs=[whole(o.shape) for o in outs],
        out_shape=outs,
        scratch_shapes=list(scratch),
        compiler_params=pltpu.CompilerParams(
            vmem_limit_bytes=min(need + room * MIB, 60 * MIB)
        ),
        cost_estimate=pl.CostEstimate(flops=1, bytes_accessed=1, transcendentals=0),
    )(*ins)


def sds(shape, dtype):
    return jax.ShapeDtypeStruct(shape, dtype)


def fill_bias(bias_ref, slope, length):
    shape = bias_ref.shape
    pos = lax.broadcasted_iota(jnp.int32, shape, 0)
    bias_ref[...] = jnp.where(pos < length, pos.astype(f32) * (slope * LOG2E), -1e30)


def diag_mask(blk):
    key = lax.broadcasted_iota(jnp.int32, (blk, blk), 0)
    query = lax.broadcasted_iota(jnp.int32, (blk, blk), 1)
    return jnp.where(key <= query, 0.0, -1e30).astype(f32)


def lane_head(shape, head_dim, which):
    lane = lax.broadcasted_iota(jnp.int32, shape, 1)
    return (lane >= which * head_dim) & (lane < (which + 1) * head_dim)


def place_pieces(dst_ref, near, far, me_ref):
    piece = dst_ref.shape[0] // 32
    for b, blocks in enumerate((near, far)):
        for n in range(4):
            row = jnp.bitwise_xor(me_ref[1], 2 * n + b)
            for k in range(4):
                at = row * 4 + jnp.bitwise_xor(me_ref[2], k)
                dst_ref[pl.ds(pl.multiple_of(at * piece, piece), piece), :] = blocks[
                    n, k * piece : (k + 1) * piece, :
                ]


def place_spread(dst_ref, blocks, me_ref):
    piece = blocks[0].shape[1]
    for k, block in enumerate(blocks):
        for r in range(8):
            at = r * 4 + jnp.bitwise_xor(me_ref[2], k)
            dst_ref[pl.ds(pl.multiple_of(at * piece, piece), piece), :] = block[r]


def unpack_small(me_ref, near, far, cuts, par_ref):
    n_small = sum(cuts)
    pieces = jnp.concatenate(
        [item[:, -16:, :n_small].reshape(64, n_small) for item in (near, far)], axis=0
    )
    seq = me_ref[2]

    def owners(cols):
        p = lax.broadcasted_iota(jnp.int32, (128, cols), 0)
        lane = lax.broadcasted_iota(jnp.int32, (128, cols), 1)
        m = ((p >> 4) & 3) * 2 + (p >> 6)
        row = jnp.bitwise_xor(m, me_ref[1])
        member = jnp.bitwise_xor((p >> 2) & 3, seq)
        return row, member, lane, (p & 3) == 0

    def spread(at, size, cols):
        one = lax.broadcasted_iota(jnp.int32, (size, cols), 0)
        two = lax.broadcasted_iota(jnp.int32, (size, cols), 1) & (size - 1)
        table = jnp.where(one == two, 1.0, 0.0).astype(bf16)
        return mm(pieces[:, at : at + size], table)

    def pick(values, mask):
        return colsum(jnp.where(mask, values, 0.0))

    starts = [sum(cuts[:i]) for i in range(len(cuts))]
    width = par_ref.shape[1]
    row, member, lane, first = owners(width)
    size = cuts[0]
    mask = first & (row * 4 + member == lane >> (size.bit_length() - 1))
    for out, i in ((0, 0), (1, 1), (2, 3), (3, 4), (4, 5), (6, 7)):
        par_ref[out : out + 1, :] = pick(spread(starts[i], size, width), mask)
    size = cuts[6]
    mask = first & (member == seq) & (row == lane >> (size.bit_length() - 1))
    par_ref[5:6, :] = pick(spread(starts[6], size, width), mask)
    par_ref[7:8, :] = jnp.zeros((1, width), f32)
    size = cuts[2]
    gw = width // 4
    row, member, lane, first = owners(gw)
    mask = first & (member == lane >> (size.bit_length() - 1))
    values = spread(starts[2], size, gw)
    return jnp.concatenate(
        [
            pick(values, mask & (row == seq)),
            jnp.zeros((1, gw), f32),
            pick(values, mask & (row == seq + 4)),
        ],
        axis=1,
    )


def pick_kernel(me_ref, wq_ref, w1_ref, small_ref, q0, q1, q2, q3, f0, f1, f2, f3):
    gw = q0.shape[1] // 3
    width = 4 * gw
    fl = w1_ref.shape[1] // 32
    dl = wq_ref.shape[0]
    for k, (out_q, out_f) in enumerate(((q0, f0), (q1, f1), (q2, f2), (q3, f3))):
        group = jnp.bitwise_xor(me_ref[0], k)
        for t in range(3):
            at = pl.multiple_of(t * width + group * gw, gw)
            out_q[:dl, t * gw : (t + 1) * gw] = wq_ref[:, pl.ds(at, gw)]
        out_q[dl:, :] = jnp.broadcast_to(small_ref[...], (16, 3 * gw))
        for r in range(8):
            at = pl.multiple_of((r * 4 + group) * fl, fl)
            out_f[:, r * fl : (r + 1) * fl] = w1_ref[:, pl.ds(at, fl)]


def attend_kernel(
    me_ref, len_ref, slope_ref, x0, x1, x2, x3, w_near, w_far, par_in, bias_in,
    att_ref, qkv_ref, norm_ref, lse_ref, par_ref, bias_ref, att_t_ref, w_ref, *, cuts,
):
    if cuts:
        bias_row = unpack_small(me_ref, w_near, w_far, cuts, par_ref)
    else:
        par_ref[...] = par_in[...]
        bias_row = bias_in[...]
    place_pieces(w_ref, w_near, w_far, me_ref)
    blk = x0.shape[0]
    seq_len, gw3 = qkv_ref.shape
    gw = gw3 // 3
    heads_here = slope_ref.shape[0]
    hd = gw // heads_here
    scale = hd ** (-0.5) * LOG2E
    me = me_ref[0]
    for k, xk in enumerate((x0, x1, x2, x3)):
        at = pl.multiple_of(jnp.bitwise_xor(me, k) * blk, blk)
        unit, _ = norm_unit(xk[...].astype(f32))
        low = (unit * par_ref[0:1, :] + par_ref[1:2, :]).astype(bf16)
        norm_ref[pl.ds(at, blk), :] = low
        qkv_ref[pl.ds(at, blk), :] = (mm(low, w_ref[...]) + bias_row).astype(bf16)
    length = len_ref[0]
    mask = diag_mask(blk)
    lse_ref[...] = jnp.zeros(lse_ref.shape, f32)
    for pair in range(heads_here // 2):
        lanes = slice(pair * 2 * hd, (pair + 1) * 2 * hd)
        keys = qkv_ref[:, gw + pair * 2 * hd : gw + (pair + 1) * 2 * hd]
        vals_t = qkv_ref[:, 2 * gw + pair * 2 * hd : 2 * gw + (pair + 1) * 2 * hd].T
        for sub in range(2):
            head = pair * 2 + sub
            fill_bias(bias_ref, slope_ref[head], length)
            for i in range(seq_len // blk):
                q_rows = slice(i * blk, (i + 1) * blk)
                q_blk = qkv_ref[q_rows, lanes]
                q_blk = jnp.where(lane_head(q_blk.shape, hd, sub), q_blk, jnp.zeros((), bf16))
                span = (i + 1) * blk
                logits = mm(keys[:span], q_blk, NT) * scale + bias_ref[:span]
                edge = logits[i * blk :] + mask
                top = jnp.max(edge, axis=0, keepdims=True)
                if i:
                    top = jnp.maximum(top, jnp.max(logits[: i * blk], axis=0, keepdims=True))
                expo = jnp.exp2(edge - top)
                total = colsum(expo)
                vt = vals_t[sub * hd : (sub + 1) * hd]
                acc = mm(vt[:, i * blk : span], expo.astype(bf16))
                if i:
                    expo = jnp.exp2(logits[: i * blk] - top)
                    total = total + colsum(expo)
                    acc = acc + mm(vt[:, : i * blk], expo.astype(bf16))
                att_t_ref[head * hd : (head + 1) * hd, q_rows] = acc / total
                lse_ref[head : head + 1, q_rows] = top + jnp.log2(total)
    att_ref[...] = att_t_ref[...].T.astype(bf16)


def feed_kernel(
    me_ref, xa, xb, a0, a1, a2, a3, ga, gb, o0, o1, o2, o3,
    u_near, u_far, w2_ref, par_ref,
    *refs, flips,
):
    if flips[1]:
        odd_ref, norm_ref, act_ref, gin_ref, sum_ref, wo_ref, w1_ref = refs
        outs = (odd_ref.at[0], odd_ref.at[1])
    else:
        far_ref, own_ref, mid_ref, wh_ref, norm_ref, act_ref, gin_ref, sum_ref = refs[:8]
        wo_ref, w1_ref = refs[8:]
        outs = (far_ref, own_ref)
    blk = xa.shape[0]
    gw = a0.shape[1]
    place_spread(wo_ref, (o0, o1, o2, o3), me_ref)
    place_pieces(w1_ref, u_near, u_far, me_ref)
    w2 = w2_ref[...].reshape(w1_ref.shape)
    me = me_ref[0]
    if not flips[1]:
        wh_ref[...] = wo_ref[pl.ds(pl.multiple_of(me * gw, gw), gw), :]
    sums = jnp.zeros(sum_ref.shape, f32)
    for n, (flip, x_ref, g_ref) in enumerate(zip(flips, (xa, xb), (ga, gb))):
        at = pl.multiple_of(jnp.bitwise_xor(me, flip) * blk, blk)
        middle = x_ref[...].astype(f32) + par_ref[2:3, :]
        for kk, ak in enumerate((a0, a1, a2, a3)):
            w_at = pl.multiple_of(jnp.bitwise_xor(me, kk) * gw, gw)
            middle = middle + mm(ak[pl.ds(at, blk), :], wo_ref[pl.ds(w_at, gw), :])
        if flip == 0:
            mid_ref[...] = middle
        unit, _ = norm_unit(middle)
        low = (unit * par_ref[3:4, :] + par_ref[4:5, :]).astype(bf16)
        rows = slice(n * blk, (n + 1) * blk)
        norm_ref[rows, :] = low
        inner = mm(low, w1_ref[...]) + par_ref[5:6, :]
        grad_act = mm(g_ref[...], w2, NT)
        square = inner * inner
        th = jnp.tanh(0.7978845608028654 * (inner + 0.044715 * inner * square))
        half = 0.5 * (1.0 + th)
        act_ref[rows, :] = (inner * half).astype(bf16)
        slope = half + (0.5 * 0.7978845608028654) * inner * (1.0 - th * th) * (
            1.0 + 3.0 * 0.044715 * square
        )
        grad_inner = (grad_act * slope).astype(bf16)
        gin_ref[rows, :] = grad_inner
        sums = sums + colsum(grad_inner.astype(f32))
        part = mm(grad_inner, w1_ref[...], NT)
        outs[n][...] = part.astype(outs[n].dtype)
    sum_ref[...] = sums


def split_rows(me_ref, send_ref, keep_ref, product):
    size = send_ref.shape[1]
    for b, out in enumerate((keep_ref, send_ref)):
        for a in range(4):
            row = jnp.bitwise_xor(me_ref[1], 2 * a + b)
            out[a] = product(pl.multiple_of(row * size, size), size).astype(bf16)


def weight_one_kernel(me_ref, na_ref, nb_ref, ga_ref, gb_ref, send_ref, keep_ref):
    split_rows(
        me_ref,
        send_ref,
        keep_ref,
        lambda at, size: mm(na_ref[:, pl.ds(at, size)], ga_ref[...], TN)
        + mm(nb_ref[:, pl.ds(at, size)], gb_ref[...], TN),
    )


def weight_two_kernel(me_ref, aa_ref, ab_ref, g3, g1, g2, g0, send_ref, keep_ref):
    blk = g0.shape[0]

    def product(at, size):
        one = aa_ref[:, pl.ds(at, size)]
        two = ab_ref[:, pl.ds(at, size)]
        return (
            mm(one[:blk], g3[...], TN)
            + mm(one[blk:], g1[...], TN)
            + mm(two[:blk], g2[...], TN)
            + mm(two[blk:], g0[...], TN)
        )

    split_rows(me_ref, send_ref, keep_ref, product)


def weight_qkv_kernel(me_ref, lhs_ref, rhs_ref, send_ref, keep_ref):
    split_rows(
        me_ref,
        send_ref,
        keep_ref,
        lambda at, size: mm(lhs_ref[:, pl.ds(at, size)], rhs_ref[...], TN),
    )


def out_weight_kernel(
    me_ref, a0, a1, a2, a3, b0, b1, b2, b3, send_ref, keep_ref, gb_ref, all_ref
):
    blk = b0.shape[0]
    gw = a0.shape[1]
    dl = send_ref.shape[1]
    for k, bk in enumerate((b0, b1, b2, b3)):
        at = pl.multiple_of(jnp.bitwise_xor(me_ref[0], k) * blk, blk)
        gb_ref[pl.ds(at, blk), :] = bk[...]
    for kk, ak in enumerate((a0, a1, a2, a3)):
        w_at = pl.multiple_of(jnp.bitwise_xor(me_ref[0], kk) * gw, gw)
        all_ref[pl.ds(w_at, gw), :] = mm(ak[...], gb_ref[...], TN)
    for b, out in enumerate((keep_ref, send_ref)):
        for a in range(4):
            at = (jnp.bitwise_xor(me_ref[1], 2 * a + b) * 4 + me_ref[0]) * dl
            out[a] = all_ref[pl.ds(pl.multiple_of(at, dl), dl), :].astype(bf16)


def add_half_kernel(keep_ref, got_ref, send_ref, left_ref):
    for n, a in enumerate((1, 3)):
        send_ref[n] = (keep_ref[a].astype(f32) + got_ref[a].astype(f32)).astype(bf16)
    for n, a in enumerate((0, 2)):
        left_ref[n] = keep_ref[a].astype(f32) + got_ref[a].astype(f32)


def add_last_kernel(left_ref, got_ref, send_ref, last_ref):
    send_ref[...] = (left_ref[1] + got_ref[1].astype(f32)).astype(bf16)
    last_ref[...] = left_ref[0] + got_ref[0].astype(f32)


def add_all_kernel(me_ref, keep_ref, got_ref, out_ref):
    for a in range(4):
        z = jnp.bitwise_xor(lax.shift_right_logical(me_ref[1], 1), a)
        out_ref[z] = (keep_ref[a].astype(f32) + got_ref[a].astype(f32)).astype(bf16)


def sum_kernel(in_ref, out_ref):
    total = in_ref[0].astype(f32)
    for n in range(1, in_ref.shape[0]):
        total = total + in_ref[n].astype(f32)
    out_ref[...] = total


def total_kernel(last_ref, *refs):
    total = last_ref[...]
    for got in refs[:-1]:
        total = total + got[...].astype(f32)
    refs[-1][...] = total


def cut_parts(me_ref, all_ref, outs):
    dl = outs[0].shape[0]
    for k, out in enumerate(outs):
        at = pl.multiple_of(jnp.bitwise_xor(me_ref[0], k) * dl, dl)
        out[...] = all_ref[pl.ds(at, dl), :].astype(out.dtype)


def parts_kernel(me_ref, one_ref, qkv_ref, o0, o1, o2, o3, all_ref):
    width = one_ref.shape[1]
    all_ref[:, :width] = one_ref[...]
    total = qkv_ref[0].astype(f32)
    for n in range(1, qkv_ref.shape[0]):
        total = total + qkv_ref[n].astype(f32)
    all_ref[:, width:] = total
    cut_parts(me_ref, all_ref, (o0, o1, o2, o3))


def spread_both_kernel(me_ref, i0, i1, i2, i3, one_ref, qkv_ref):
    pieces = (i0, i1, i2, i3)
    width = one_ref.shape[1] // 4
    for out_ref, base, size in ((one_ref, 0, width // 8), (qkv_ref, width, width // 4)):
        for k, piece in enumerate(pieces):
            for t in range(out_ref.shape[1] // (4 * size)):
                at = (t * 4 + jnp.bitwise_xor(me_ref[0], k)) * size
                out_ref[:, pl.ds(pl.multiple_of(at, size), size)] = piece[
                    :, base + t * size : base + (t + 1) * size
                ].astype(f32)


def pack_small_kernel(me_ref, one_ref, two_ref, ba_ref, bb_ref, col_ref, out_ref, *, cuts):
    count = out_ref.shape[0]
    width = one_ref.shape[1]
    gw = width // 4

    def fold(values, size, owner, cols):
        lane = lax.broadcasted_iota(jnp.int32, (count, cols), 1)
        device = lax.broadcasted_iota(jnp.int32, (count, cols), 0)
        mine = jnp.where(owner(lane >> (size.bit_length() - 1), device), values, 0.0)
        one = lax.broadcasted_iota(jnp.int32, (cols, size), 0) & (size - 1)
        two = lax.broadcasted_iota(jnp.int32, (cols, size), 1)
        table = jnp.where(one == two, 1.0, 0.0).astype(f32)
        return lax.dot_general(
            mine, table, NN, precision=lax.Precision.HIGHEST, preferred_element_type=f32
        )

    def plain(values):
        return fold(values, cuts[0], lambda part, device: part == device, width)

    member = me_ref[0]
    query = fold(col_ref[:, :gw], cuts[2], lambda p, d: p + 4 * member == d, gw)
    value = fold(col_ref[:, 2 * gw :], cuts[2], lambda p, d: p + 4 * member + 16 == d, gw)
    hidden = fold(ba_ref[...] + bb_ref[...], cuts[6], lambda p, d: p * 4 + member == d, width)
    out_ref[...] = jnp.concatenate(
        [
            plain(one_ref[0:1, :]),
            plain(one_ref[1:2, :]),
            query + value,
            plain(two_ref[2:3, :]),
            plain(two_ref[0:1, :]),
            plain(two_ref[1:2, :]),
            hidden,
            plain(two_ref[3:4, :]),
        ],
        axis=1,
    )


def mlp_kernel(aa_ref, ab_ref, w2_ref, odd_ref, far_ref, own_ref):
    blk = own_ref.shape[0]
    w2 = w2_ref[...].reshape(aa_ref.shape[1], own_ref.shape[1])
    odd_ref[0] = mm(aa_ref[:blk], w2).astype(bf16)
    odd_ref[1] = mm(aa_ref[blk:], w2).astype(bf16)
    far_ref[...] = mm(ab_ref[:blk], w2)
    own_ref[...] = mm(ab_ref[blk:], w2)


def middle_kernel(own, near, far, mid_ref, g0, par_ref, gb_ref, gm_ref, sum_ref):
    upstream = own[...] + near[1].astype(f32) + far[...].astype(f32)
    unit, inv = norm_unit(mid_ref[...])
    grad_mlp = g0[...].astype(f32)
    grad_middle = grad_mlp + norm_back(upstream, unit, inv, par_ref[3:4, :])
    low = grad_middle.astype(bf16)
    gm_ref[...] = grad_middle
    gb_ref[...] = low
    sum_ref[0:1, :] = colsum(upstream * unit)
    sum_ref[1:2, :] = colsum(upstream)
    sum_ref[2:3, :] = colsum(low.astype(f32))
    sum_ref[3:4, :] = colsum(grad_mlp)


def back_kernel(
    me_ref, len_ref, slope_ref, b0, b1, b2, b3, wh_ref, qkv_ref, lse_ref,
    dqkv_ref, ga_ref, bias_ref, dk_ref, dv_ref, dqt_ref,
):
    blk = b0.shape[0]
    seq_len, gw3 = qkv_ref.shape
    gw = gw3 // 3
    heads_here = slope_ref.shape[0]
    hd = gw // heads_here
    scale = hd ** (-0.5)
    me = me_ref[0]
    w_heads = wh_ref[...]
    for k, bk in enumerate((b0, b1, b2, b3)):
        at = pl.multiple_of(jnp.bitwise_xor(me, k) * blk, blk)
        ga_ref[pl.ds(at, blk), :] = mm(bk[...], w_heads, NT).astype(bf16)
    length = len_ref[0]
    mask = diag_mask(blk)
    none = jnp.zeros((), bf16)
    for pair in range(heads_here // 2):
        lanes = slice(pair * 2 * hd, (pair + 1) * 2 * hd)
        k_lanes = slice(gw + pair * 2 * hd, gw + (pair + 1) * 2 * hd)
        v_lanes = slice(2 * gw + pair * 2 * hd, 2 * gw + (pair + 1) * 2 * hd)
        keys = qkv_ref[:, k_lanes]
        keys_t = keys.T
        vals = qkv_ref[:, v_lanes]
        dk_ref[...] = jnp.zeros(dk_ref.shape, f32)
        dv_ref[...] = jnp.zeros(dv_ref.shape, f32)
        for sub in range(2):
            head = pair * 2 + sub
            fill_bias(bias_ref, slope_ref[head], length)
            for i in range(seq_len // blk):
                q_rows = slice(i * blk, (i + 1) * blk)
                span = (i + 1) * blk
                pick = lane_head((blk, 2 * hd), hd, sub)
                q_blk = jnp.where(pick, qkv_ref[q_rows, lanes], none)
                g_blk = jnp.where(pick, ga_ref[q_rows, lanes], none)
                logits = mm(keys[:span], q_blk, NT) * (scale * LOG2E) + bias_ref[:span]
                lse = lse_ref[head : head + 1, q_rows]
                edge = jnp.exp2(logits[i * blk :] + mask - lse)
                if i:
                    soft = jnp.concatenate([jnp.exp2(logits[: i * blk] - lse), edge], axis=0)
                else:
                    soft = edge
                grad_soft = mm(vals[:span], g_blk, NT)
                row_dot = colsum(soft * grad_soft)
                grad_scores = (soft * (grad_soft - row_dot)).astype(bf16)
                soft_low = soft.astype(bf16)
                dv_ref[:span] += mm(soft_low, g_blk)
                dk_ref[:span] += mm(grad_scores, q_blk)
                dqt_ref[sub * hd : (sub + 1) * hd, q_rows] = mm(
                    keys_t[sub * hd : (sub + 1) * hd, :span], grad_scores
                )
        dqkv_ref[:, lanes] = (dqt_ref[...].T * scale).astype(bf16)
        dqkv_ref[:, k_lanes] = (dk_ref[...] * scale).astype(bf16)
        dqkv_ref[:, v_lanes] = dv_ref[...].astype(bf16)


def first_norm_kernel(
    me_ref, x0, x1, x2, x3, dqkv_ref, w_near, w_far,
    odd_ref, far_ref, own_ref, sum_ref, col_ref, w_ref,
):
    blk = x0.shape[0]
    place_pieces(w_ref, w_near, w_far, me_ref)
    me = me_ref[0]
    gain = jnp.zeros((1, x0.shape[1]), f32)
    shift = gain
    cols = jnp.zeros(col_ref.shape, f32)
    for k in (3, 2, 1, 0):
        xk = (x0, x1, x2, x3)[k]
        out = (own_ref, odd_ref.at[1], far_ref, odd_ref.at[0])[k]
        at = pl.multiple_of(jnp.bitwise_xor(me, k) * blk, blk)
        grad = dqkv_ref[pl.ds(at, blk), :]
        part = mm(grad, w_ref[...], NT)
        out[...] = part.astype(out.dtype)
        unit, _ = norm_unit(xk[...].astype(f32))
        gain = gain + colsum(part * unit)
        shift = shift + colsum(part)
        cols = cols + colsum(grad.astype(f32))
    sum_ref[0:1, :] = gain
    sum_ref[1:2, :] = shift
    col_ref[...] = cols


def input_kernel(own, near, far, x_ref, gm_ref, par_ref, out_ref):
    upstream = own[...] + near[1].astype(f32) + far[...].astype(f32)
    unit, inv = norm_unit(x_ref[...].astype(f32))
    out_ref[...] = (gm_ref[...] + norm_back(upstream, unit, inv, par_ref[0:1, :])).astype(bf16)


def head_slopes(count):
    return jnp.exp2(-8.0 * (jnp.arange(count, dtype=f32) + 1.0) / count)


def per_device(
    layer_in,
    grad_out,
    lengths,
    ln1_gain,
    ln1_shift,
    w_qkv,
    b_qv,
    w_out,
    b_out,
    ln2_gain,
    ln2_shift,
    w_fc1,
    b_fc1,
    w_fc2,
    b_fc2,
):
    rows = lax.axis_size("rows")
    groups = lax.axis_size("seq")
    everyone = rows * groups
    my_group = lax.axis_index("seq")
    my_row = lax.axis_index("rows")
    blk = layer_in.shape[1]
    width = layer_in.shape[2]
    seq_len = blk * groups
    heads_here = HEADS // groups
    gw = width // groups
    dl = w_qkv.shape[0]
    fl = w_fc2.shape[0]
    hidden = rows * fl
    cut = width // 8
    assert groups == 4 and hidden == width
    direct = rows == 8
    me = jnp.stack([my_group, my_row, my_group]).astype(jnp.int32)
    if not direct:
        me = me * jnp.array([1, 0, 0], jnp.int32)

    def swap(values, flip):
        return lax.ppermute(values, "seq", [(i, i ^ flip) for i in range(groups)])

    def swap_x(values):
        return lax.ppermute(values, "rows", [(i, i ^ 1) for i in range(rows)])

    def swap_z(values, flip):
        return lax.ppermute(values, "rows", [(i, i ^ (2 * flip)) for i in range(rows)])

    def exchange_z(values):
        return lax.all_to_all(
            values,
            "rows",
            split_axis=0,
            concat_axis=0,
            axis_index_groups=[[2 * z + x for z in range(rows // 2)] for x in range(2)],
            tiled=True,
        )

    def gather_z(values):
        return [values] + [swap_z(values, a) for a in (1, 2, 3)]

    def after(values, *others):
        return lax.optimization_barrier((values, *others))[0]

    def gather_seq(values):
        far = swap(values, 2)
        return [values, swap(values, 1), far, swap(far, 1)]

    def far_sum(far, near):
        return (far + near[0].astype(f32)).astype(bf16)

    parts = [ln1_gain, ln1_shift, b_qv, b_out, ln2_gain, ln2_shift, b_fc1, b_fc2]
    cuts = tuple(part.shape[0] for part in parts)
    n_small = sum(cuts)
    small = jnp.zeros((1, 3 * gw), bf16)
    at = 0
    for part in parts:
        n = part.shape[0]
        small = small + jnp.pad(part.reshape(1, n), ((0, 0), (at, 3 * gw - at - n)))
        at += n

    if direct:
        w2_all = jnp.concatenate([w_fc2, w_out], axis=0)
        w2_all = lax.all_gather(w2_all, "rows", axis=0, tiled=False)
        picked = call(
            pick_kernel,
            (me, w_qkv, w_fc1, small),
            [SMEM, whole(w_qkv.shape), whole(w_fc1.shape), whole(small.shape)],
            [sds((dl + 16, 3 * gw), bf16)] * 4 + [sds((dl, hidden), bf16)] * 4,
        )
        got = [picked[0]] + [swap(picked[k], k) for k in (1, 2, 3)]
        wq_block = jnp.concatenate(
            [item[:dl] for item in got] + [item[dl : dl + 4] for item in got], axis=0
        )
        wq_z = gather_z(wq_block)
        picked_late = [after(item, wq_block) for item in picked[4:]]
        w1_block = jnp.concatenate(
            [picked_late[0]] + [swap(picked_late[k], k) for k in (1, 2, 3)], axis=0
        )
        x_own = after(layer_in[0], w1_block)
    else:
        wq_parts = w_qkv.reshape(dl, 3, groups, gw).transpose(2, 0, 1, 3)
        f1_parts = w_fc1.reshape(dl, rows, groups, fl).transpose(2, 0, 1, 3)
        stage = jnp.concatenate(
            [f1_parts.reshape(groups, dl, hidden), wq_parts.reshape(groups, dl, 3 * gw)], axis=2
        )
        stage = lax.all_to_all(stage, "seq", split_axis=0, concat_axis=0, tiled=True)
        stage = lax.all_gather(
            stage.reshape(groups * dl, hidden + 3 * gw), "rows", axis=0, tiled=True
        )
        stage = stage.reshape(4, 2, cut, hidden + 3 * gw)
        w1_near, w1_far = stage[:, 0, :, :hidden], stage[:, 1, :, :hidden]
        wq_near, wq_far = stage[:, 0, :, hidden:], stage[:, 1, :, hidden:]
        w2_all = lax.all_gather(w_fc2, "rows", axis=0, tiled=True).reshape(8, cut, width)
        wo_mine = lax.all_gather(w_out, "rows", axis=0, tiled=False)
        wo_mine = wo_mine.reshape(8, width // 32, width)
        x_own = layer_in[0]
    par = jnp.zeros((8, width), f32)
    bias_mine = jnp.zeros((1, 3 * gw), f32)
    if not direct:
        full = lax.all_gather(small[:, :n_small], ("rows", "seq"), axis=0, tiled=True).astype(f32)
        ends = [sum(cuts[: i + 1]) for i in range(len(cuts))]
        full = [full[:, e - n : e].reshape(1, -1) for e, n in zip(ends, cuts)]
        bqv = lax.dynamic_index_in_dim(
            full[2].reshape(2, groups, gw), my_group, 1, keepdims=False
        )
        bias_mine = jnp.concatenate([bqv[0:1], jnp.zeros((1, gw), f32), bqv[1:2]], axis=1)
        bfc1 = lax.dynamic_index_in_dim(
            full[6].reshape(rows, groups, fl), my_group, 1, keepdims=False
        ).reshape(1, hidden)
        par = jnp.concatenate(
            [full[0], full[1], full[3], full[4], full[5], bfc1, full[7], full[7]], axis=0
        )

    positions = my_group * blk + jnp.arange(blk, dtype=jnp.int32)
    live_own = (positions < lengths[0])[:, None]
    x_far = swap(x_own, 2)
    x_near = swap(x_own, 1)
    g_own = jnp.where(live_own, grad_out[0], jnp.zeros((), bf16))
    if direct:
        wq_near = after(jnp.stack(wq_z), x_near, x_far)
        wq_far = swap_x(wq_near)
        x_far = after(x_far, wq_near)
        w1_z = gather_z(after(w1_block, wq_near))
        g_own = after(g_own, wq_near)
    g_far = swap(g_own, 2)
    xs = [x_own, x_near, x_far, swap(x_far, 1)]
    slopes = lax.dynamic_slice_in_dim(head_slopes(HEADS), my_group * heads_here, heads_here)

    x_spec = whole((blk, width))
    odd_spec = whole((2, blk, width))
    a_spec = whole((seq_len, gw))
    par_spec = whole((8, width))
    wq_spec = whole(wq_near.shape)
    w_spec = whole((4, cut, width))
    w2_spec = pl.BlockSpec((8, cut, width), lambda *_: (0, 0, 0))
    wo_spec = whole((8, width // 32, width))
    qkv_spec = whole((seq_len, 3 * gw))
    act_shape = (seq_len, width)
    half_shape = (2 * blk, width)

    att, qkv, normed, lse, par = call(
        functools.partial(attend_kernel, cuts=cuts if direct else ()),
        (me, lengths, slopes, *xs, wq_near, wq_far, par, bias_mine),
        [SMEM] * 3 + [x_spec] * 4 + [wq_spec] * 2 + [par_spec, whole((1, 3 * gw))],
        [
            sds((seq_len, gw), bf16),
            sds((seq_len, 3 * gw), bf16),
            sds(act_shape, bf16),
            sds((8, seq_len), f32),
            sds((8, width), f32),
        ],
        [
            pltpu.VMEM((seq_len, blk), f32),
            pltpu.VMEM((gw, seq_len), f32),
            pltpu.VMEM((width, 3 * gw), bf16),
        ],
    )
    atts = gather_seq(att)
    if direct:
        w1_near = jnp.stack([after(item, att) for item in w1_z])
        w1_far = swap_x(w1_near)
        wo_mine = after(w2_all, att)[:, cut:]
    wos = gather_seq(wo_mine)
    g_near, g_far = after(g_own, att), after(g_far, att)
    gs = [g_own, swap(g_near, 1), g_far, swap(g_far, 1)]
    if not direct:
        wo_all = jnp.stack(wos)[jnp.arange(4, dtype=jnp.int32) ^ my_group]
        wo_all = wo_all.reshape(4, rows, dl, width).transpose(1, 0, 2, 3)
        wo_all = wo_all.reshape(8, 4, width // 32, width)
        wos = [wo_all[:, k] for k in range(4)]


    def feed(flips, outs):
        return call(
            functools.partial(feed_kernel, flips=flips),
            (
                me, *(xs[k] for k in flips), *atts, *(gs[k] for k in flips), *wos, w1_near, w1_far,
                w2_all, par,
            ),
            [SMEM] + [x_spec] * 2 + [a_spec] * 4 + [x_spec] * 2 + [wo_spec] * 4 + [w_spec] * 2
            + [w2_spec, par_spec],
            outs + [sds(half_shape, bf16)] * 3 + [sds((1, width), f32)],
            [pltpu.VMEM((width, width), bf16)] * 2,
        )

    odd_list = [sds((2, blk, width), bf16)]
    even_list = [sds((blk, width), f32)] * 2
    odd, norm_a, act_a, gin_a, bsum_a = feed((3, 1), odd_list)
    near = swap(odd, 1)
    xs = [after(item, odd) for item in xs]
    far, own, middle, w_heads, norm_b, act_b, gin_b, bsum_b = feed(
        (2, 0), even_list + [sds((blk, width), f32), sds((gw, width), bf16)]
    )
    far = far_sum(far, near)
    act_b = after(act_b, far)
    far = swap(far, 2)
    half_spec = whole(half_shape)
    split_list = [sds((4, cut, width), bf16)] * 2
    one_send, one_keep = call(
        weight_one_kernel,
        (me, after(norm_a, act_b), norm_b, gin_a, gin_b),
        [SMEM] + [half_spec] * 4,
        split_list,
    )
    two_send, two_keep = call(
        weight_two_kernel,
        (me, act_a, after(act_b, one_keep), gs[3], gs[1], gs[2], gs[0]),
        [SMEM] + [half_spec] * 2 + [x_spec] * 4,
        split_list,
    )
    gb, grad_middle, sums_two = call(
        middle_kernel,
        (after(own, two_keep), near, far, middle, gs[0], par),
        [x_spec, odd_spec] + [x_spec] * 3 + [par_spec],
        [sds((blk, width), bf16), sds((blk, width), f32), sds((4, width), f32)],
    )
    m_odd, m_far, m_own = call(
        mlp_kernel,
        (after(act_a, gb), act_b, w2_all),
        [half_spec] * 2 + [w2_spec],
        odd_list + even_list,
    )
    gb_far = after(swap(gb, 2), m_own)
    gbs = [gb, swap(gb, 1), gb_far, swap(gb_far, 1)]

    def add_half(send, keep, late):
        size, cols = keep.shape[1:]
        return call(
            add_half_kernel,
            (after(keep, late), swap_x(send)),
            [whole(keep.shape)] * 2,
            [sds((2, size, cols), bf16), sds((2, size, cols), f32)],
        )

    def add_last(halves, *late):
        send, left = halves
        size, cols = left.shape[1:]
        return call(
            add_last_kernel,
            (after(left, *late), swap_z(send, 1)),
            [whole(left.shape)] * 2,
            [sds((size, cols), bf16), sds((size, cols), f32)],
        )

    def add_all(send, keep, *late):
        return call(
            add_all_kernel,
            (me, after(keep, *late), swap_x(send)),
            [SMEM] + [whole(keep.shape)] * 2,
            [sds(keep.shape, bf16)],
        )[0]

    def sum_z(values, late):
        size, cols = values.shape[1:]
        return call(
            sum_kernel,
            (after(values, late),),
            [whole(values.shape)],
            [sds((size, cols), f32)],
        )[0]

    def total(ins, late):
        spec = whole(ins[0].shape)
        return call(
            total_kernel,
            (after(ins[0], late), *ins[1:]),
            [spec] * len(ins),
            [sds(ins[0].shape, f32)],
        )[0]

    m_near = swap(m_odd, 1)
    late = m_own
    if direct:
        one_half = add_half(one_send, one_keep, gbs[2])
        late = one_half[1]
    (dqkv,) = call(
        back_kernel,
        (me, lengths, slopes, after(gbs[0], late), *gbs[1:], w_heads, qkv, lse),
        [SMEM] * 3 + [x_spec] * 5 + [qkv_spec, whole((8, seq_len))],
        [sds((seq_len, 3 * gw), bf16)],
        [
            pltpu.VMEM((seq_len, gw), bf16),
            pltpu.VMEM((seq_len, blk), f32),
            pltpu.VMEM((seq_len, gw // 2), f32),
            pltpu.VMEM((seq_len, gw // 2), f32),
            pltpu.VMEM((gw // 2, seq_len), f32),
        ],
    )
    late = dqkv
    if direct:
        one_last = add_last(one_half, dqkv, m_near)
        late = one_last[1]

    n_odd, n_far, n_own, sums_one, cols = call(
        first_norm_kernel,
        (me, *xs, after(dqkv, late), wq_near, wq_far),
        [SMEM] + [x_spec] * 4 + [qkv_spec] + [wq_spec] * 2,
        odd_list + even_list + [sds((2, width), f32), sds((1, 3 * gw), f32)],
        [pltpu.VMEM((width, 3 * gw), bf16)],
    )
    n_near = swap(n_odd, 1)
    late = n_own
    dq_send, dq_keep = call(
        weight_qkv_kernel,
        (me, normed, after(dqkv, late)),
        [SMEM, whole(act_shape), qkv_spec],
        [sds((4, cut, 3 * gw), bf16)] * 2,
    )
    if direct:
        two_half = add_half(two_send, two_keep, dq_keep)
        late = two_half[1]
    n_far = far_sum(after(n_far, late), n_near)
    late = n_far
    n_far = swap(n_far, 2)

    if direct:
        (small_grads,) = call(
            functools.partial(pack_small_kernel, cuts=cuts),
            (me, after(sums_one, late), sums_two, bsum_a, bsum_b, cols),
            [SMEM]
            + [whole(item.shape) for item in (sums_one, sums_two, bsum_a, bsum_b, cols)],
            [sds((everyone, n_small), f32)],
        )
    else:
        mine = (jnp.arange(groups) == my_group).astype(f32)
        bqv_sums = jnp.concatenate([cols[:, :gw], cols[:, 2 * gw :]], axis=0)
        grad_bqv = mine[None, :, None] * bqv_sums[:, None, :]
        grad_bfc1 = mine[None, :, None] * (bsum_a + bsum_b).reshape(rows, 1, fl)
        small_grads = jnp.concatenate(
            [
                part.reshape(everyone, -1)
                for part in (
                    sums_one[0],
                    sums_one[1],
                    grad_bqv,
                    sums_two[2],
                    sums_two[0],
                    sums_two[1],
                    grad_bfc1,
                    sums_two[3],
                )
            ],
            axis=1,
        )
    late = small_grads
    small_grads = lax.all_to_all(
        small_grads, ("rows", "seq"), split_axis=0, concat_axis=0, tiled=True
    )
    s_small = jnp.sum(small_grads, axis=0)
    m_far = far_sum(after(m_far, late), m_near)
    late = m_far
    m_far = swap(m_far, 2)

    def parts_of(values):
        cols = values.shape[-1]
        total = jnp.sum(values.reshape(rows, 4, dl, cols).astype(f32), axis=0).astype(bf16)
        return [
            lax.dynamic_index_in_dim(total, my_group ^ k, 0, keepdims=False) for k in range(4)
        ]

    def spread(pieces, parts):
        pieces = [pieces[0]] + [swap(pieces[k], k) for k in (1, 2, 3)]
        size = pieces[0].shape[1] // parts
        order = jnp.arange(4, dtype=jnp.int32) ^ my_group
        stacked = jnp.stack(pieces)[order].reshape(4, dl, parts, size)
        return stacked.transpose(1, 2, 0, 3).reshape(dl, 4 * parts * size).astype(f32)

    if direct:
        out_send, out_keep = call(
            out_weight_kernel,
            (me, *atts, after(gbs[0], late), *gbs[1:]),
            [SMEM] + [a_spec] * 4 + [x_spec] * 4,
            [sds((4, dl, width), bf16)] * 2,
            [pltpu.VMEM((seq_len, width), bf16), pltpu.VMEM((width, width), f32)],
        )
        one_total = total((one_last[1], swap_z(one_last[0], 2)), out_keep)
        qkv_all = add_all(dq_send, dq_keep, one_total, s_small)
        late = qkv_all
        qkv_all = exchange_z(qkv_all)
        two_last = add_last(two_half, late)
        out_all = add_all(out_send, out_keep, two_last[1])
        late = out_all
    (grad_input,) = call(
        input_kernel,
        (after(n_own, late), n_near, n_far, layer_in[0], grad_middle, par),
        [x_spec, odd_spec] + [x_spec] * 3 + [par_spec],
        [sds((blk, width), bf16)],
    )
    if not direct:

        def rows_sum(send, keep):
            both = jnp.stack([keep, send], axis=1).reshape(rows, -1, keep.shape[-1])
            return lax.all_to_all(both, "rows", split_axis=0, concat_axis=0, tiled=True)

        one_parts = parts_of(rows_sum(one_send, one_keep))
        qkv_parts = parts_of(rows_sum(dq_send, dq_keep))
        s_wfc2 = jnp.sum(rows_sum(two_send, two_keep).astype(f32), axis=0)
        order = jnp.arange(4, dtype=jnp.int32) ^ my_group
        att_full = jnp.stack(atts)[order].transpose(1, 0, 2).reshape(seq_len, width)
        gb_full = jnp.stack(gbs)[order].reshape(seq_len, width)
        dw_out = mm(att_full, gb_full, TN).astype(bf16).reshape(rows, groups, dl, width)
        dw_out = lax.dynamic_index_in_dim(dw_out, my_group, 1, keepdims=False)
        got_out = lax.all_to_all(dw_out, "rows", split_axis=0, concat_axis=0, tiled=True)
        s_wout = jnp.sum(got_out.astype(f32), axis=0)
    mlp_own = m_own + m_near[1].astype(f32) + m_far.astype(f32)
    layer_result = jnp.where(live_own, middle + mlp_own + par[6:7], 0.0).astype(bf16)

    if direct:
        parts_ins = (after(one_total, grad_input, layer_result), qkv_all)
        pieces = call(
            parts_kernel,
            (me, *parts_ins),
            [SMEM, whole((cut, width)), whole(qkv_all.shape)],
            [sds((dl, width + 3 * gw), bf16)] * 4,
            [pltpu.VMEM((cut, width + 3 * gw), f32)],
        )
        out_all = exchange_z(after(out_all, pieces[0]))
        s_wfc2 = total((two_last[1], swap_z(two_last[0], 2)), pieces[0])
        pieces = [after(pieces[0], s_wfc2)] + [swap(pieces[k], k) for k in (1, 2, 3)]
        s_wfc1, s_wqkv = call(
            spread_both_kernel,
            (me, *pieces),
            [SMEM] + [whole(pieces[0].shape)] * 4,
            [sds((dl, 4 * width), f32), sds((dl, 3 * width), f32)],
        )
        s_wout = sum_z(out_all, s_wqkv)
    else:
        s_wfc1 = spread(one_parts, rows)
        s_wqkv = spread(qkv_parts, 3)

    smalls = []
    at = 0
    for n in cuts:
        smalls.append(s_small[at : at + n])
        at += n
    (s_gain_one, s_shift_one, s_bqv, s_bout, s_gain_two, s_shift_two, s_bfc1, s_bfc2) = smalls
    return (
        layer_result[None],
        grad_input[None],
        s_gain_one,
        s_shift_one,
        s_wqkv,
        s_bqv,
        s_wout,
        s_bout,
        s_gain_two,
        s_shift_two,
        s_wfc1,
        s_bfc1,
        s_wfc2,
        s_bfc2,
    )


def solution(mesh):
    both = P(("rows", "seq"))
    wide = P(("rows", "seq"), None)
    acts = P("rows", "seq", None)
    in_specs = (
        acts,
        acts,
        P("rows"),
        both,
        both,
        wide,
        both,
        wide,
        both,
        both,
        both,
        wide,
        both,
        wide,
        both,
    )
    out_specs = (
        acts,
        acts,
        both,
        both,
        wide,
        both,
        wide,
        both,
        both,
        both,
        wide,
        both,
        wide,
        both,
    )
    return jax.shard_map(
        per_device, mesh=mesh, in_specs=in_specs, out_specs=out_specs, check_vma=False
    )
```

```python
import functools
import math

import jax
import jax.numpy as jnp
from jax import lax
from jax.experimental import pallas as pl
from jax.experimental.pallas import tpu as pltpu
from jax.sharding import PartitionSpec as P

HEADS = 16


EPS = 1e-05
LOG2E = 1.4426950408889634
f32 = jnp.float32
bf16 = jnp.bfloat16
MIB = 1024 * 1024

NN = (((1,), (0,)), ((), ()))
NT = (((1,), (1,)), ((), ()))
TN = (((0,), (0,)), ((), ()))


def mm(a, b, dims=NN):
    return lax.dot_general(a, b, dims, preferred_element_type=f32)


def norm_unit(values):
    average = jnp.mean(values, axis=-1, keepdims=True)
    centred = values - average
    inv_std = lax.rsqrt(jnp.mean(centred * centred, axis=-1, keepdims=True) + EPS)
    return centred * inv_std, inv_std


def norm_back(upstream, unit_rows, inv_std, gain_vec):
    scaled = upstream * gain_vec
    part_one = jnp.mean(scaled, axis=-1, keepdims=True)
    part_two = jnp.mean(scaled * unit_rows, axis=-1, keepdims=True)
    return inv_std * (scaled - part_one - unit_rows * part_two)


def colsum(values):
    return jnp.sum(values, axis=0, keepdims=True)


def whole(shape):
    return pl.BlockSpec(shape, lambda *_: (0,) * len(shape))


SMEM = pl.BlockSpec(memory_space=pltpu.SMEM)


def size_of(item):
    return math.prod(item.shape) * jnp.dtype(item.dtype).itemsize


def call(body, ins, in_specs, outs, scratch=(), room=6):
    blocks = [(item, spec) for item, spec in zip(ins, in_specs) if spec is not SMEM]
    need = sum(size_of(item) for item, _ in blocks) + sum(size_of(o) for o in outs)
    need += sum(size_of(item) for item in scratch)
    return pl.pallas_call(
        body,
        grid=(1,),
        in_specs=in_specs,
        out_specs=[whole(o.shape) for o in outs],
        out_shape=outs,
        scratch_shapes=list(scratch),
        compiler_params=pltpu.CompilerParams(
            vmem_limit_bytes=min(need + room * MIB, 60 * MIB)
        ),
        cost_estimate=pl.CostEstimate(flops=1, bytes_accessed=1, transcendentals=0),
    )(*ins)


def sds(shape, dtype):
    return jax.ShapeDtypeStruct(shape, dtype)


def fill_bias(bias_ref, slope, length):
    shape = bias_ref.shape
    pos = lax.broadcasted_iota(jnp.int32, shape, 0)
    bias_ref[...] = jnp.where(pos < length, pos.astype(f32) * (slope * LOG2E), -1e30)


def diag_mask(blk):
    key = lax.broadcasted_iota(jnp.int32, (blk, blk), 0)
    query = lax.broadcasted_iota(jnp.int32, (blk, blk), 1)
    return jnp.where(key <= query, 0.0, -1e30).astype(f32)


def lane_head(shape, head_dim, which):
    lane = lax.broadcasted_iota(jnp.int32, shape, 1)
    return (lane >= which * head_dim) & (lane < (which + 1) * head_dim)


def place_pieces(dst_ref, near, far, me_ref):
    piece = dst_ref.shape[0] // 32
    for b, blocks in enumerate((near, far)):
        for n in range(4):
            row = jnp.bitwise_xor(me_ref[1], 2 * n + b)
            for k in range(4):
                at = row * 4 + jnp.bitwise_xor(me_ref[2], k)
                dst_ref[pl.ds(pl.multiple_of(at * piece, piece), piece), :] = blocks[
                    n, k * piece : (k + 1) * piece, :
                ]


def place_spread(dst_ref, blocks, me_ref):
    piece = blocks[0].shape[1]
    for k, block in enumerate(blocks):
        for r in range(8):
            at = r * 4 + jnp.bitwise_xor(me_ref[2], k)
            dst_ref[pl.ds(pl.multiple_of(at * piece, piece), piece), :] = block[r]


def unpack_small(me_ref, near, far, cuts, par_ref):
    n_small = sum(cuts)
    pieces = jnp.concatenate(
        [item[:, -16:, :n_small].reshape(64, n_small) for item in (near, far)], axis=0
    )
    seq = me_ref[2]

    def owners(cols):
        p = lax.broadcasted_iota(jnp.int32, (128, cols), 0)
        lane = lax.broadcasted_iota(jnp.int32, (128, cols), 1)
        m = ((p >> 4) & 3) * 2 + (p >> 6)
        row = jnp.bitwise_xor(m, me_ref[1])
        member = jnp.bitwise_xor((p >> 2) & 3, seq)
        return row, member, lane, (p & 3) == 0

    def spread(at, size, cols):
        one = lax.broadcasted_iota(jnp.int32, (size, cols), 0)
        two = lax.broadcasted_iota(jnp.int32, (size, cols), 1) & (size - 1)
        table = jnp.where(one == two, 1.0, 0.0).astype(bf16)
        return mm(pieces[:, at : at + size], table)

    def pick(values, mask):
        return colsum(jnp.where(mask, values, 0.0))

    starts = [sum(cuts[:i]) for i in range(len(cuts))]
    width = par_ref.shape[1]
    row, member, lane, first = owners(width)
    size = cuts[0]
    mask = first & (row * 4 + member == lane >> (size.bit_length() - 1))
    for out, i in ((0, 0), (1, 1), (2, 3), (3, 4), (4, 5), (6, 7)):
        par_ref[out : out + 1, :] = pick(spread(starts[i], size, width), mask)
    size = cuts[6]
    mask = first & (member == seq) & (row == lane >> (size.bit_length() - 1))
    par_ref[5:6, :] = pick(spread(starts[6], size, width), mask)
    par_ref[7:8, :] = jnp.zeros((1, width), f32)
    size = cuts[2]
    gw = width // 4
    row, member, lane, first = owners(gw)
    mask = first & (member == lane >> (size.bit_length() - 1))
    values = spread(starts[2], size, gw)
    return jnp.concatenate(
        [
            pick(values, mask & (row == seq)),
            jnp.zeros((1, gw), f32),
            pick(values, mask & (row == seq + 4)),
        ],
        axis=1,
    )


def pick_kernel(me_ref, wq_ref, w1_ref, small_ref, q0, q1, q2, q3, f0, f1, f2, f3):
    gw = q0.shape[1] // 3
    width = 4 * gw
    fl = w1_ref.shape[1] // 32
    dl = wq_ref.shape[0]
    for k, (out_q, out_f) in enumerate(((q0, f0), (q1, f1), (q2, f2), (q3, f3))):
        group = jnp.bitwise_xor(me_ref[0], k)
        for t in range(3):
            at = pl.multiple_of(t * width + group * gw, gw)
            out_q[:dl, t * gw : (t + 1) * gw] = wq_ref[:, pl.ds(at, gw)]
        out_q[dl:, :] = jnp.broadcast_to(small_ref[...], (16, 3 * gw))
        for r in range(8):
            at = pl.multiple_of((r * 4 + group) * fl, fl)
            out_f[:, r * fl : (r + 1) * fl] = w1_ref[:, pl.ds(at, fl)]


def attend_kernel(
    me_ref, len_ref, slope_ref, x0, x1, x2, x3, w_near, w_far, par_in, bias_in,
    att_ref, qkv_ref, norm_ref, lse_ref, par_ref, bias_ref, att_t_ref, w_ref, *, cuts,
):
    if cuts:
        bias_row = unpack_small(me_ref, w_near, w_far, cuts, par_ref)
    else:
        par_ref[...] = par_in[...]
        bias_row = bias_in[...]
    place_pieces(w_ref, w_near, w_far, me_ref)
    blk = x0.shape[0]
    seq_len, gw3 = qkv_ref.shape
    gw = gw3 // 3
    heads_here = slope_ref.shape[0]
    hd = gw // heads_here
    scale = hd ** (-0.5) * LOG2E
    me = me_ref[0]
    for k, xk in enumerate((x0, x1, x2, x3)):
        at = pl.multiple_of(jnp.bitwise_xor(me, k) * blk, blk)
        unit, _ = norm_unit(xk[...].astype(f32))
        low = (unit * par_ref[0:1, :] + par_ref[1:2, :]).astype(bf16)
        norm_ref[pl.ds(at, blk), :] = low
        qkv_ref[pl.ds(at, blk), :] = (mm(low, w_ref[...]) + bias_row).astype(bf16)
    length = len_ref[0]
    mask = diag_mask(blk)
    lse_ref[...] = jnp.zeros(lse_ref.shape, f32)
    for pair in range(heads_here // 2):
        lanes = slice(pair * 2 * hd, (pair + 1) * 2 * hd)
        keys = qkv_ref[:, gw + pair * 2 * hd : gw + (pair + 1) * 2 * hd]
        vals_t = qkv_ref[:, 2 * gw + pair * 2 * hd : 2 * gw + (pair + 1) * 2 * hd].T
        for sub in range(2):
            head = pair * 2 + sub
            fill_bias(bias_ref, slope_ref[head], length)
            for i in range(seq_len // blk):
                q_rows = slice(i * blk, (i + 1) * blk)
                q_blk = qkv_ref[q_rows, lanes]
                q_blk = jnp.where(lane_head(q_blk.shape, hd, sub), q_blk, jnp.zeros((), bf16))
                span = (i + 1) * blk
                logits = mm(keys[:span], q_blk, NT) * scale + bias_ref[:span]
                edge = logits[i * blk :] + mask
                top = jnp.max(edge, axis=0, keepdims=True)
                if i:
                    top = jnp.maximum(top, jnp.max(logits[: i * blk], axis=0, keepdims=True))
                expo = jnp.exp2(edge - top)
                total = colsum(expo)
                vt = vals_t[sub * hd : (sub + 1) * hd]
                acc = mm(vt[:, i * blk : span], expo.astype(bf16))
                if i:
                    expo = jnp.exp2(logits[: i * blk] - top)
                    total = total + colsum(expo)
                    acc = acc + mm(vt[:, : i * blk], expo.astype(bf16))
                att_t_ref[head * hd : (head + 1) * hd, q_rows] = acc / total
                lse_ref[head : head + 1, q_rows] = top + jnp.log2(total)
    att_ref[...] = att_t_ref[...].T.astype(bf16)


def feed_kernel(
    me_ref, xa, xb, a0, a1, a2, a3, ga, gb, o0, o1, o2, o3,
    u_near, u_far, w2_ref, par_ref,
    *refs, flips,
):
    if flips[1]:
        odd_ref, norm_ref, act_ref, gin_ref, sum_ref, wo_ref, w1_ref = refs
        outs = (odd_ref.at[0], odd_ref.at[1])
    else:
        far_ref, own_ref, mid_ref, wh_ref, norm_ref, act_ref, gin_ref, sum_ref = refs[:8]
        wo_ref, w1_ref = refs[8:]
        outs = (far_ref, own_ref)
    blk = xa.shape[0]
    gw = a0.shape[1]
    place_spread(wo_ref, (o0, o1, o2, o3), me_ref)
    place_pieces(w1_ref, u_near, u_far, me_ref)
    w2 = w2_ref[...].reshape(w1_ref.shape)
    me = me_ref[0]
    if not flips[1]:
        wh_ref[...] = wo_ref[pl.ds(pl.multiple_of(me * gw, gw), gw), :]
    sums = jnp.zeros(sum_ref.shape, f32)
    for n, (flip, x_ref, g_ref) in enumerate(zip(flips, (xa, xb), (ga, gb))):
        at = pl.multiple_of(jnp.bitwise_xor(me, flip) * blk, blk)
        middle = x_ref[...].astype(f32) + par_ref[2:3, :]
        for kk, ak in enumerate((a0, a1, a2, a3)):
            w_at = pl.multiple_of(jnp.bitwise_xor(me, kk) * gw, gw)
            middle = middle + mm(ak[pl.ds(at, blk), :], wo_ref[pl.ds(w_at, gw), :])
        if flip == 0:
            mid_ref[...] = middle
        unit, _ = norm_unit(middle)
        low = (unit * par_ref[3:4, :] + par_ref[4:5, :]).astype(bf16)
        rows = slice(n * blk, (n + 1) * blk)
        norm_ref[rows, :] = low
        inner = mm(low, w1_ref[...]) + par_ref[5:6, :]
        grad_act = mm(g_ref[...], w2, NT)
        square = inner * inner
        th = jnp.tanh(0.7978845608028654 * (inner + 0.044715 * inner * square))
        half = 0.5 * (1.0 + th)
        act_ref[rows, :] = (inner * half).astype(bf16)
        slope = half + (0.5 * 0.7978845608028654) * inner * (1.0 - th * th) * (
            1.0 + 3.0 * 0.044715 * square
        )
        grad_inner = (grad_act * slope).astype(bf16)
        gin_ref[rows, :] = grad_inner
        sums = sums + colsum(grad_inner.astype(f32))
        part = mm(grad_inner, w1_ref[...], NT)
        outs[n][...] = part.astype(outs[n].dtype)
    sum_ref[...] = sums


def split_rows(me_ref, send_ref, keep_ref, product):
    size = send_ref.shape[1]
    for b, out in enumerate((keep_ref, send_ref)):
        for a in range(4):
            row = jnp.bitwise_xor(me_ref[1], 2 * a + b)
            out[a] = product(pl.multiple_of(row * size, size), size).astype(bf16)


def weight_one_kernel(me_ref, na_ref, nb_ref, ga_ref, gb_ref, send_ref, keep_ref):
    split_rows(
        me_ref,
        send_ref,
        keep_ref,
        lambda at, size: mm(na_ref[:, pl.ds(at, size)], ga_ref[...], TN)
        + mm(nb_ref[:, pl.ds(at, size)], gb_ref[...], TN),
    )


def weight_two_kernel(me_ref, aa_ref, ab_ref, g3, g1, g2, g0, send_ref, keep_ref):
    blk = g0.shape[0]

    def product(at, size):
        one = aa_ref[:, pl.ds(at, size)]
        two = ab_ref[:, pl.ds(at, size)]
        return (
            mm(one[:blk], g3[...], TN)
            + mm(one[blk:], g1[...], TN)
            + mm(two[:blk], g2[...], TN)
            + mm(two[blk:], g0[...], TN)
        )

    split_rows(me_ref, send_ref, keep_ref, product)


def weight_qkv_kernel(me_ref, lhs_ref, rhs_ref, send_ref, keep_ref):
    split_rows(
        me_ref,
        send_ref,
        keep_ref,
        lambda at, size: mm(lhs_ref[:, pl.ds(at, size)], rhs_ref[...], TN),
    )


def out_weight_kernel(
    me_ref, a0, a1, a2, a3, b0, b1, b2, b3, send_ref, keep_ref, gb_ref, all_ref
):
    blk = b0.shape[0]
    gw = a0.shape[1]
    dl = send_ref.shape[1]
    for k, bk in enumerate((b0, b1, b2, b3)):
        at = pl.multiple_of(jnp.bitwise_xor(me_ref[0], k) * blk, blk)
        gb_ref[pl.ds(at, blk), :] = bk[...]
    for kk, ak in enumerate((a0, a1, a2, a3)):
        w_at = pl.multiple_of(jnp.bitwise_xor(me_ref[0], kk) * gw, gw)
        all_ref[pl.ds(w_at, gw), :] = mm(ak[...], gb_ref[...], TN)
    for b, out in enumerate((keep_ref, send_ref)):
        for a in range(4):
            at = (jnp.bitwise_xor(me_ref[1], 2 * a + b) * 4 + me_ref[0]) * dl
            out[a] = all_ref[pl.ds(pl.multiple_of(at, dl), dl), :].astype(bf16)


def add_half_kernel(keep_ref, got_ref, send_ref, left_ref):
    for n, a in enumerate((1, 3)):
        send_ref[n] = (keep_ref[a].astype(f32) + got_ref[a].astype(f32)).astype(bf16)
    for n, a in enumerate((0, 2)):
        left_ref[n] = keep_ref[a].astype(f32) + got_ref[a].astype(f32)


def add_last_kernel(left_ref, got_ref, send_ref, last_ref):
    send_ref[...] = (left_ref[1] + got_ref[1].astype(f32)).astype(bf16)
    last_ref[...] = left_ref[0] + got_ref[0].astype(f32)


def add_all_kernel(me_ref, keep_ref, got_ref, out_ref):
    for a in range(4):
        z = jnp.bitwise_xor(lax.shift_right_logical(me_ref[1], 1), a)
        out_ref[z] = (keep_ref[a].astype(f32) + got_ref[a].astype(f32)).astype(bf16)


def add_split_kernel(keep_ref, got_ref, t0_ref, t1_ref, t2_ref, t3_ref):
    for a, out in enumerate((t0_ref, t1_ref, t2_ref, t3_ref)):
        out[...] = (keep_ref[a].astype(f32) + got_ref[a].astype(f32)).astype(out.dtype)


def total_kernel(last_ref, *refs):
    total = last_ref[...]
    for got in refs[:-1]:
        total = total + got[...].astype(f32)
    refs[-1][...] = total


def cut_parts(me_ref, all_ref, outs):
    dl = outs[0].shape[0]
    for k, out in enumerate(outs):
        at = pl.multiple_of(jnp.bitwise_xor(me_ref[0], k) * dl, dl)
        out[...] = all_ref[pl.ds(at, dl), :].astype(out.dtype)


def parts_kernel(me_ref, one_ref, qkv_ref, o0, o1, o2, o3, all_ref):
    width = one_ref.shape[1]
    all_ref[:, :width] = one_ref[...]
    total = qkv_ref[0].astype(f32)
    for n in range(1, qkv_ref.shape[0]):
        total = total + qkv_ref[n].astype(f32)
    all_ref[:, width:] = total
    cut_parts(me_ref, all_ref, (o0, o1, o2, o3))


def spread_both_kernel(me_ref, i0, i1, i2, i3, one_ref, qkv_ref):
    pieces = (i0, i1, i2, i3)
    width = one_ref.shape[1] // 4
    for out_ref, base, size in ((one_ref, 0, width // 8), (qkv_ref, width, width // 4)):
        for k, piece in enumerate(pieces):
            for t in range(out_ref.shape[1] // (4 * size)):
                at = (t * 4 + jnp.bitwise_xor(me_ref[0], k)) * size
                out_ref[:, pl.ds(pl.multiple_of(at, size), size)] = piece[
                    :, base + t * size : base + (t + 1) * size
                ].astype(f32)


def pack_small_kernel(me_ref, one_ref, two_ref, ba_ref, bb_ref, col_ref, out_ref, *, cuts):
    count = out_ref.shape[0]
    width = one_ref.shape[1]
    gw = width // 4

    def fold(values, size, owner, cols):
        lane = lax.broadcasted_iota(jnp.int32, (count, cols), 1)
        device = lax.broadcasted_iota(jnp.int32, (count, cols), 0)
        mine = jnp.where(owner(lane >> (size.bit_length() - 1), device), values, 0.0)
        one = lax.broadcasted_iota(jnp.int32, (cols, size), 0) & (size - 1)
        two = lax.broadcasted_iota(jnp.int32, (cols, size), 1)
        table = jnp.where(one == two, 1.0, 0.0).astype(f32)
        return lax.dot_general(
            mine, table, NN, precision=lax.Precision.HIGHEST, preferred_element_type=f32
        )

    def plain(values):
        return fold(values, cuts[0], lambda part, device: part == device, width)

    member = me_ref[0]
    query = fold(col_ref[:, :gw], cuts[2], lambda p, d: p + 4 * member == d, gw)
    value = fold(col_ref[:, 2 * gw :], cuts[2], lambda p, d: p + 4 * member + 16 == d, gw)
    hidden = fold(ba_ref[...] + bb_ref[...], cuts[6], lambda p, d: p * 4 + member == d, width)
    out_ref[...] = jnp.concatenate(
        [
            plain(one_ref[0:1, :]),
            plain(one_ref[1:2, :]),
            query + value,
            plain(two_ref[2:3, :]),
            plain(two_ref[0:1, :]),
            plain(two_ref[1:2, :]),
            hidden,
            plain(two_ref[3:4, :]),
        ],
        axis=1,
    )


def mlp_kernel(aa_ref, ab_ref, w2_ref, odd_ref, far_ref, own_ref):
    blk = own_ref.shape[0]
    w2 = w2_ref[...].reshape(aa_ref.shape[1], own_ref.shape[1])
    odd_ref[0] = mm(aa_ref[:blk], w2).astype(bf16)
    odd_ref[1] = mm(aa_ref[blk:], w2).astype(bf16)
    far_ref[...] = mm(ab_ref[:blk], w2)
    own_ref[...] = mm(ab_ref[blk:], w2)


def middle_kernel(own, near, far, mid_ref, g0, par_ref, gb_ref, gm_ref, sum_ref):
    upstream = own[...] + near[1].astype(f32) + far[...].astype(f32)
    unit, inv = norm_unit(mid_ref[...])
    grad_mlp = g0[...].astype(f32)
    grad_middle = grad_mlp + norm_back(upstream, unit, inv, par_ref[3:4, :])
    low = grad_middle.astype(bf16)
    gm_ref[...] = grad_middle
    gb_ref[...] = low
    sum_ref[0:1, :] = colsum(upstream * unit)
    sum_ref[1:2, :] = colsum(upstream)
    sum_ref[2:3, :] = colsum(low.astype(f32))
    sum_ref[3:4, :] = colsum(grad_mlp)


def back_kernel(
    me_ref, len_ref, slope_ref, b0, b1, b2, b3, wh_ref, qkv_ref, lse_ref,
    dqkv_ref, ga_ref, bias_ref, dk_ref, dv_ref, dqt_ref,
):
    blk = b0.shape[0]
    seq_len, gw3 = qkv_ref.shape
    gw = gw3 // 3
    heads_here = slope_ref.shape[0]
    hd = gw // heads_here
    scale = hd ** (-0.5)
    me = me_ref[0]
    w_heads = wh_ref[...]
    for k, bk in enumerate((b0, b1, b2, b3)):
        at = pl.multiple_of(jnp.bitwise_xor(me, k) * blk, blk)
        ga_ref[pl.ds(at, blk), :] = mm(bk[...], w_heads, NT).astype(bf16)
    length = len_ref[0]
    mask = diag_mask(blk)
    none = jnp.zeros((), bf16)
    for pair in range(heads_here // 2):
        lanes = slice(pair * 2 * hd, (pair + 1) * 2 * hd)
        k_lanes = slice(gw + pair * 2 * hd, gw + (pair + 1) * 2 * hd)
        v_lanes = slice(2 * gw + pair * 2 * hd, 2 * gw + (pair + 1) * 2 * hd)
        keys = qkv_ref[:, k_lanes]
        keys_t = keys.T
        vals = qkv_ref[:, v_lanes]
        dk_ref[...] = jnp.zeros(dk_ref.shape, f32)
        dv_ref[...] = jnp.zeros(dv_ref.shape, f32)
        for sub in range(2):
            head = pair * 2 + sub
            fill_bias(bias_ref, slope_ref[head], length)
            for i in range(seq_len // blk):
                q_rows = slice(i * blk, (i + 1) * blk)
                span = (i + 1) * blk
                pick = lane_head((blk, 2 * hd), hd, sub)
                q_blk = jnp.where(pick, qkv_ref[q_rows, lanes], none)
                g_blk = jnp.where(pick, ga_ref[q_rows, lanes], none)
                logits = mm(keys[:span], q_blk, NT) * (scale * LOG2E) + bias_ref[:span]
                lse = lse_ref[head : head + 1, q_rows]
                edge = jnp.exp2(logits[i * blk :] + mask - lse)
                if i:
                    soft = jnp.concatenate([jnp.exp2(logits[: i * blk] - lse), edge], axis=0)
                else:
                    soft = edge
                grad_soft = mm(vals[:span], g_blk, NT)
                row_dot = colsum(soft * grad_soft)
                grad_scores = (soft * (grad_soft - row_dot)).astype(bf16)
                soft_low = soft.astype(bf16)
                dv_ref[:span] += mm(soft_low, g_blk)
                dk_ref[:span] += mm(grad_scores, q_blk)
                dqt_ref[sub * hd : (sub + 1) * hd, q_rows] = mm(
                    keys_t[sub * hd : (sub + 1) * hd, :span], grad_scores
                )
        dqkv_ref[:, lanes] = (dqt_ref[...].T * scale).astype(bf16)
        dqkv_ref[:, k_lanes] = (dk_ref[...] * scale).astype(bf16)
        dqkv_ref[:, v_lanes] = dv_ref[...].astype(bf16)


def first_norm_kernel(
    me_ref, x0, x1, x2, x3, dqkv_ref, w_near, w_far,
    odd_ref, far_ref, own_ref, sum_ref, col_ref, w_ref,
):
    blk = x0.shape[0]
    place_pieces(w_ref, w_near, w_far, me_ref)
    me = me_ref[0]
    gain = jnp.zeros((1, x0.shape[1]), f32)
    shift = gain
    cols = jnp.zeros(col_ref.shape, f32)
    for k in (3, 2, 1, 0):
        xk = (x0, x1, x2, x3)[k]
        out = (own_ref, odd_ref.at[1], far_ref, odd_ref.at[0])[k]
        at = pl.multiple_of(jnp.bitwise_xor(me, k) * blk, blk)
        grad = dqkv_ref[pl.ds(at, blk), :]
        part = mm(grad, w_ref[...], NT)
        out[...] = part.astype(out.dtype)
        unit, _ = norm_unit(xk[...].astype(f32))
        gain = gain + colsum(part * unit)
        shift = shift + colsum(part)
        cols = cols + colsum(grad.astype(f32))
    sum_ref[0:1, :] = gain
    sum_ref[1:2, :] = shift
    col_ref[...] = cols


def input_kernel(own, near, far, x_ref, gm_ref, par_ref, out_ref):
    upstream = own[...] + near[1].astype(f32) + far[...].astype(f32)
    unit, inv = norm_unit(x_ref[...].astype(f32))
    out_ref[...] = (gm_ref[...] + norm_back(upstream, unit, inv, par_ref[0:1, :])).astype(bf16)


def head_slopes(count):
    return jnp.exp2(-8.0 * (jnp.arange(count, dtype=f32) + 1.0) / count)


def per_device(
    layer_in,
    grad_out,
    lengths,
    ln1_gain,
    ln1_shift,
    w_qkv,
    b_qv,
    w_out,
    b_out,
    ln2_gain,
    ln2_shift,
    w_fc1,
    b_fc1,
    w_fc2,
    b_fc2,
):
    rows = lax.axis_size("rows")
    groups = lax.axis_size("seq")
    everyone = rows * groups
    my_group = lax.axis_index("seq")
    my_row = lax.axis_index("rows")
    blk = layer_in.shape[1]
    width = layer_in.shape[2]
    seq_len = blk * groups
    heads_here = HEADS // groups
    gw = width // groups
    dl = w_qkv.shape[0]
    fl = w_fc2.shape[0]
    hidden = rows * fl
    cut = width // 8
    assert groups == 4 and hidden == width
    direct = rows == 8
    me = jnp.stack([my_group, my_row, my_group]).astype(jnp.int32)
    if not direct:
        me = me * jnp.array([1, 0, 0], jnp.int32)

    def swap(values, flip):
        return lax.ppermute(values, "seq", [(i, i ^ flip) for i in range(groups)])

    def swap_x(values):
        return lax.ppermute(values, "rows", [(i, i ^ 1) for i in range(rows)])

    def swap_z(values, flip):
        return lax.ppermute(values, "rows", [(i, i ^ (2 * flip)) for i in range(rows)])

    def exchange_z(values):
        return lax.all_to_all(
            values,
            "rows",
            split_axis=0,
            concat_axis=0,
            axis_index_groups=[[2 * z + x for z in range(rows // 2)] for x in range(2)],
            tiled=True,
        )

    def gather_z(values):
        return [values] + [swap_z(values, a) for a in (1, 2, 3)]

    def after(values, *others):
        return lax.optimization_barrier((values, *others))[0]

    def gather_seq(values):
        far = swap(values, 2)
        return [values, swap(values, 1), far, swap(far, 1)]

    def far_sum(far, near):
        return (far + near[0].astype(f32)).astype(bf16)

    parts = [ln1_gain, ln1_shift, b_qv, b_out, ln2_gain, ln2_shift, b_fc1, b_fc2]
    cuts = tuple(part.shape[0] for part in parts)
    n_small = sum(cuts)
    small = jnp.zeros((1, 3 * gw), bf16)
    at = 0
    for part in parts:
        n = part.shape[0]
        small = small + jnp.pad(part.reshape(1, n), ((0, 0), (at, 3 * gw - at - n)))
        at += n

    if direct:
        w2_all = jnp.concatenate([w_fc2, w_out], axis=0)
        w2_all = lax.all_gather(w2_all, "rows", axis=0, tiled=False)
        picked = call(
            pick_kernel,
            (me, w_qkv, w_fc1, small),
            [SMEM, whole(w_qkv.shape), whole(w_fc1.shape), whole(small.shape)],
            [sds((dl + 16, 3 * gw), bf16)] * 4 + [sds((dl, hidden), bf16)] * 4,
        )
        got = [picked[0]] + [swap(picked[k], k) for k in (1, 2, 3)]
        wq_block = jnp.concatenate(
            [item[:dl] for item in got] + [item[dl : dl + 4] for item in got], axis=0
        )
        wq_z = gather_z(wq_block)
        picked_late = [after(item, wq_block) for item in picked[4:]]
        w1_block = jnp.concatenate(
            [picked_late[0]] + [swap(picked_late[k], k) for k in (1, 2, 3)], axis=0
        )
        x_own = after(layer_in[0], w1_block)
    else:
        wq_parts = w_qkv.reshape(dl, 3, groups, gw).transpose(2, 0, 1, 3)
        f1_parts = w_fc1.reshape(dl, rows, groups, fl).transpose(2, 0, 1, 3)
        stage = jnp.concatenate(
            [f1_parts.reshape(groups, dl, hidden), wq_parts.reshape(groups, dl, 3 * gw)], axis=2
        )
        stage = lax.all_to_all(stage, "seq", split_axis=0, concat_axis=0, tiled=True)
        stage = lax.all_gather(
            stage.reshape(groups * dl, hidden + 3 * gw), "rows", axis=0, tiled=True
        )
        stage = stage.reshape(4, 2, cut, hidden + 3 * gw)
        w1_near, w1_far = stage[:, 0, :, :hidden], stage[:, 1, :, :hidden]
        wq_near, wq_far = stage[:, 0, :, hidden:], stage[:, 1, :, hidden:]
        w2_all = lax.all_gather(w_fc2, "rows", axis=0, tiled=True).reshape(8, cut, width)
        wo_mine = lax.all_gather(w_out, "rows", axis=0, tiled=False)
        wo_mine = wo_mine.reshape(8, width // 32, width)
        x_own = layer_in[0]
    par = jnp.zeros((8, width), f32)
    bias_mine = jnp.zeros((1, 3 * gw), f32)
    if not direct:
        full = lax.all_gather(small[:, :n_small], ("rows", "seq"), axis=0, tiled=True).astype(f32)
        ends = [sum(cuts[: i + 1]) for i in range(len(cuts))]
        full = [full[:, e - n : e].reshape(1, -1) for e, n in zip(ends, cuts)]
        bqv = lax.dynamic_index_in_dim(
            full[2].reshape(2, groups, gw), my_group, 1, keepdims=False
        )
        bias_mine = jnp.concatenate([bqv[0:1], jnp.zeros((1, gw), f32), bqv[1:2]], axis=1)
        bfc1 = lax.dynamic_index_in_dim(
            full[6].reshape(rows, groups, fl), my_group, 1, keepdims=False
        ).reshape(1, hidden)
        par = jnp.concatenate(
            [full[0], full[1], full[3], full[4], full[5], bfc1, full[7], full[7]], axis=0
        )

    positions = my_group * blk + jnp.arange(blk, dtype=jnp.int32)
    live_own = (positions < lengths[0])[:, None]
    x_far = swap(x_own, 2)
    x_near = swap(x_own, 1)
    g_own = jnp.where(live_own, grad_out[0], jnp.zeros((), bf16))
    if direct:
        wq_near = after(jnp.stack(wq_z), x_near, x_far)
        wq_far = swap_x(wq_near)
        x_far = after(x_far, wq_near)
        w1_z = gather_z(after(w1_block, wq_near))
        g_own = after(g_own, wq_near)
    g_far = swap(g_own, 2)
    xs = [x_own, x_near, x_far, swap(x_far, 1)]
    slopes = lax.dynamic_slice_in_dim(head_slopes(HEADS), my_group * heads_here, heads_here)

    x_spec = whole((blk, width))
    odd_spec = whole((2, blk, width))
    a_spec = whole((seq_len, gw))
    par_spec = whole((8, width))
    wq_spec = whole(wq_near.shape)
    w_spec = whole((4, cut, width))
    w2_spec = pl.BlockSpec((8, cut, width), lambda *_: (0, 0, 0))
    wo_spec = whole((8, width // 32, width))
    qkv_spec = whole((seq_len, 3 * gw))
    act_shape = (seq_len, width)
    half_shape = (2 * blk, width)

    att, qkv, normed, lse, par = call(
        functools.partial(attend_kernel, cuts=cuts if direct else ()),
        (me, lengths, slopes, *xs, wq_near, wq_far, par, bias_mine),
        [SMEM] * 3 + [x_spec] * 4 + [wq_spec] * 2 + [par_spec, whole((1, 3 * gw))],
        [
            sds((seq_len, gw), bf16),
            sds((seq_len, 3 * gw), bf16),
            sds(act_shape, bf16),
            sds((8, seq_len), f32),
            sds((8, width), f32),
        ],
        [
            pltpu.VMEM((seq_len, blk), f32),
            pltpu.VMEM((gw, seq_len), f32),
            pltpu.VMEM((width, 3 * gw), bf16),
        ],
    )
    atts = gather_seq(att)
    if direct:
        w1_near = jnp.stack([after(item, att) for item in w1_z])
        w1_far = swap_x(w1_near)
        wo_mine = after(w2_all, att)[:, cut:]
    wos = gather_seq(wo_mine)
    g_near, g_far = after(g_own, att), after(g_far, att)
    gs = [g_own, swap(g_near, 1), g_far, swap(g_far, 1)]
    if not direct:
        wo_all = jnp.stack(wos)[jnp.arange(4, dtype=jnp.int32) ^ my_group]
        wo_all = wo_all.reshape(4, rows, dl, width).transpose(1, 0, 2, 3)
        wo_all = wo_all.reshape(8, 4, width // 32, width)
        wos = [wo_all[:, k] for k in range(4)]


    def feed(flips, outs):
        return call(
            functools.partial(feed_kernel, flips=flips),
            (
                me, *(xs[k] for k in flips), *atts, *(gs[k] for k in flips), *wos, w1_near, w1_far,
                w2_all, par,
            ),
            [SMEM] + [x_spec] * 2 + [a_spec] * 4 + [x_spec] * 2 + [wo_spec] * 4 + [w_spec] * 2
            + [w2_spec, par_spec],
            outs + [sds(half_shape, bf16)] * 3 + [sds((1, width), f32)],
            [pltpu.VMEM((width, width), bf16)] * 2,
        )

    odd_list = [sds((2, blk, width), bf16)]
    even_list = [sds((blk, width), f32)] * 2
    odd, norm_a, act_a, gin_a, bsum_a = feed((3, 1), odd_list)
    near = swap(odd, 1)
    xs = [after(item, odd) for item in xs]
    far, own, middle, w_heads, norm_b, act_b, gin_b, bsum_b = feed(
        (2, 0), even_list + [sds((blk, width), f32), sds((gw, width), bf16)]
    )
    far = far_sum(far, near)
    act_b = after(act_b, far)
    far = swap(far, 2)
    half_spec = whole(half_shape)
    split_list = [sds((4, cut, width), bf16)] * 2
    one_send, one_keep = call(
        weight_one_kernel,
        (me, after(norm_a, act_b), norm_b, gin_a, gin_b),
        [SMEM] + [half_spec] * 4,
        split_list,
    )
    two_send, two_keep = call(
        weight_two_kernel,
        (me, act_a, after(act_b, one_keep), gs[3], gs[1], gs[2], gs[0]),
        [SMEM] + [half_spec] * 2 + [x_spec] * 4,
        split_list,
    )
    gb, grad_middle, sums_two = call(
        middle_kernel,
        (after(own, two_keep), near, far, middle, gs[0], par),
        [x_spec, odd_spec] + [x_spec] * 3 + [par_spec],
        [sds((blk, width), bf16), sds((blk, width), f32), sds((4, width), f32)],
    )
    m_odd, m_far, m_own = call(
        mlp_kernel,
        (after(act_a, gb), act_b, w2_all),
        [half_spec] * 2 + [w2_spec],
        odd_list + even_list,
    )
    gb_far = after(swap(gb, 2), m_own)
    gbs = [gb, swap(gb, 1), gb_far, swap(gb_far, 1)]

    def add_half(send, keep, late):
        size, cols = keep.shape[1:]
        return call(
            add_half_kernel,
            (after(keep, late), swap_x(send)),
            [whole(keep.shape)] * 2,
            [sds((2, size, cols), bf16), sds((2, size, cols), f32)],
        )

    def add_last(halves, *late):
        send, left = halves
        size, cols = left.shape[1:]
        return call(
            add_last_kernel,
            (after(left, *late), swap_z(send, 1)),
            [whole(left.shape)] * 2,
            [sds((size, cols), bf16), sds((size, cols), f32)],
        )

    def add_all(send, keep, *late):
        return call(
            add_all_kernel,
            (me, after(keep, *late), swap_x(send)),
            [SMEM] + [whole(keep.shape)] * 2,
            [sds(keep.shape, bf16)],
        )[0]

    def add_split(send, keep, late):
        size, cols = keep.shape[1:]
        last, *sends = call(
            add_split_kernel,
            (after(keep, late), swap_x(send)),
            [whole(keep.shape)] * 2,
            [sds((size, cols), f32)] + [sds((size, cols), bf16)] * 3,
        )
        return (last, *(swap_z(item, a) for a, item in zip((1, 2, 3), sends)))

    def total(ins, late):
        spec = whole(ins[0].shape)
        return call(
            total_kernel,
            (after(ins[0], late), *ins[1:]),
            [spec] * len(ins),
            [sds(ins[0].shape, f32)],
        )[0]

    m_near = swap(m_odd, 1)
    late = m_own
    if direct:
        one_half = add_half(one_send, one_keep, gbs[2])
        late = one_half[1]
    (dqkv,) = call(
        back_kernel,
        (me, lengths, slopes, after(gbs[0], late), *gbs[1:], w_heads, qkv, lse),
        [SMEM] * 3 + [x_spec] * 5 + [qkv_spec, whole((8, seq_len))],
        [sds((seq_len, 3 * gw), bf16)],
        [
            pltpu.VMEM((seq_len, gw), bf16),
            pltpu.VMEM((seq_len, blk), f32),
            pltpu.VMEM((seq_len, gw // 2), f32),
            pltpu.VMEM((seq_len, gw // 2), f32),
            pltpu.VMEM((gw // 2, seq_len), f32),
        ],
    )
    late = dqkv
    if direct:
        one_last = add_last(one_half, dqkv, m_near)
        late = one_last[1]

    n_odd, n_far, n_own, sums_one, cols = call(
        first_norm_kernel,
        (me, *xs, after(dqkv, late), wq_near, wq_far),
        [SMEM] + [x_spec] * 4 + [qkv_spec] + [wq_spec] * 2,
        odd_list + even_list + [sds((2, width), f32), sds((1, 3 * gw), f32)],
        [pltpu.VMEM((width, 3 * gw), bf16)],
    )
    n_near = swap(n_odd, 1)
    late = n_own
    dq_send, dq_keep = call(
        weight_qkv_kernel,
        (me, normed, after(dqkv, late)),
        [SMEM, whole(act_shape), qkv_spec],
        [sds((4, cut, 3 * gw), bf16)] * 2,
    )
    if direct:
        two_half = add_half(two_send, two_keep, dq_keep)
        late = two_half[1]
    n_far = far_sum(after(n_far, late), n_near)
    late = n_far
    n_far = swap(n_far, 2)

    if direct:
        (small_grads,) = call(
            functools.partial(pack_small_kernel, cuts=cuts),
            (me, after(sums_one, late), sums_two, bsum_a, bsum_b, cols),
            [SMEM]
            + [whole(item.shape) for item in (sums_one, sums_two, bsum_a, bsum_b, cols)],
            [sds((everyone, n_small), f32)],
        )
    else:
        mine = (jnp.arange(groups) == my_group).astype(f32)
        bqv_sums = jnp.concatenate([cols[:, :gw], cols[:, 2 * gw :]], axis=0)
        grad_bqv = mine[None, :, None] * bqv_sums[:, None, :]
        grad_bfc1 = mine[None, :, None] * (bsum_a + bsum_b).reshape(rows, 1, fl)
        small_grads = jnp.concatenate(
            [
                part.reshape(everyone, -1)
                for part in (
                    sums_one[0],
                    sums_one[1],
                    grad_bqv,
                    sums_two[2],
                    sums_two[0],
                    sums_two[1],
                    grad_bfc1,
                    sums_two[3],
                )
            ],
            axis=1,
        )
    late = small_grads
    small_grads = lax.all_to_all(
        small_grads, ("rows", "seq"), split_axis=0, concat_axis=0, tiled=True
    )
    s_small = jnp.sum(small_grads, axis=0)
    m_far = far_sum(after(m_far, late), m_near)
    late = m_far
    m_far = swap(m_far, 2)

    def parts_of(values):
        cols = values.shape[-1]
        total = jnp.sum(values.reshape(rows, 4, dl, cols).astype(f32), axis=0).astype(bf16)
        return [
            lax.dynamic_index_in_dim(total, my_group ^ k, 0, keepdims=False) for k in range(4)
        ]

    def spread(pieces, parts):
        pieces = [pieces[0]] + [swap(pieces[k], k) for k in (1, 2, 3)]
        size = pieces[0].shape[1] // parts
        order = jnp.arange(4, dtype=jnp.int32) ^ my_group
        stacked = jnp.stack(pieces)[order].reshape(4, dl, parts, size)
        return stacked.transpose(1, 2, 0, 3).reshape(dl, 4 * parts * size).astype(f32)

    if direct:
        out_send, out_keep = call(
            out_weight_kernel,
            (me, *atts, after(gbs[0], late), *gbs[1:]),
            [SMEM] + [a_spec] * 4 + [x_spec] * 4,
            [sds((4, dl, width), bf16)] * 2,
            [pltpu.VMEM((seq_len, width), bf16), pltpu.VMEM((width, width), f32)],
        )
        one_total = total((one_last[1], swap_z(one_last[0], 2)), out_keep)
        two_last = add_last(two_half, one_total)
        qkv_all = add_all(dq_send, dq_keep, two_last[1], s_small)
        out_all = add_split(out_send, out_keep, qkv_all)
        qkv_all = exchange_z(qkv_all)
        late = out_all[0]
    (grad_input,) = call(
        input_kernel,
        (after(n_own, late), n_near, n_far, layer_in[0], grad_middle, par),
        [x_spec, odd_spec] + [x_spec] * 3 + [par_spec],
        [sds((blk, width), bf16)],
    )
    if not direct:

        def rows_sum(send, keep):
            both = jnp.stack([keep, send], axis=1).reshape(rows, -1, keep.shape[-1])
            return lax.all_to_all(both, "rows", split_axis=0, concat_axis=0, tiled=True)

        one_parts = parts_of(rows_sum(one_send, one_keep))
        qkv_parts = parts_of(rows_sum(dq_send, dq_keep))
        s_wfc2 = jnp.sum(rows_sum(two_send, two_keep).astype(f32), axis=0)
        order = jnp.arange(4, dtype=jnp.int32) ^ my_group
        att_full = jnp.stack(atts)[order].transpose(1, 0, 2).reshape(seq_len, width)
        gb_full = jnp.stack(gbs)[order].reshape(seq_len, width)
        dw_out = mm(att_full, gb_full, TN).astype(bf16).reshape(rows, groups, dl, width)
        dw_out = lax.dynamic_index_in_dim(dw_out, my_group, 1, keepdims=False)
        got_out = lax.all_to_all(dw_out, "rows", split_axis=0, concat_axis=0, tiled=True)
        s_wout = jnp.sum(got_out.astype(f32), axis=0)
    mlp_own = m_own + m_near[1].astype(f32) + m_far.astype(f32)
    layer_result = jnp.where(live_own, middle + mlp_own + par[6:7], 0.0).astype(bf16)

    if direct:
        s_wfc2 = total((two_last[1], swap_z(two_last[0], 2)), grad_input)
        s_wout = total(out_all, s_wfc2)
        parts_ins = (after(one_total, s_wout), qkv_all)
        pieces = call(
            parts_kernel,
            (me, *parts_ins),
            [SMEM, whole((cut, width)), whole(qkv_all.shape)],
            [sds((dl, width + 3 * gw), bf16)] * 4,
            [pltpu.VMEM((cut, width + 3 * gw), f32)],
        )
        pieces = [pieces[0]] + [swap(pieces[k], k) for k in (1, 2, 3)]
        s_wfc1, s_wqkv = call(
            spread_both_kernel,
            (me, *pieces),
            [SMEM] + [whole(pieces[0].shape)] * 4,
            [sds((dl, 4 * width), f32), sds((dl, 3 * width), f32)],
        )
    else:
        s_wfc1 = spread(one_parts, rows)
        s_wqkv = spread(qkv_parts, 3)

    smalls = []
    at = 0
    for n in cuts:
        smalls.append(s_small[at : at + n])
        at += n
    (s_gain_one, s_shift_one, s_bqv, s_bout, s_gain_two, s_shift_two, s_bfc1, s_bfc2) = smalls
    return (
        layer_result[None],
        grad_input[None],
        s_gain_one,
        s_shift_one,
        s_wqkv,
        s_bqv,
        s_wout,
        s_bout,
        s_gain_two,
        s_shift_two,
        s_wfc1,
        s_bfc1,
        s_wfc2,
        s_bfc2,
    )


def solution(mesh):
    both = P(("rows", "seq"))
    wide = P(("rows", "seq"), None)
    acts = P("rows", "seq", None)
    in_specs = (
        acts,
        acts,
        P("rows"),
        both,
        both,
        wide,
        both,
        wide,
        both,
        both,
        both,
        wide,
        both,
        wide,
        both,
    )
    out_specs = (
        acts,
        acts,
        both,
        both,
        wide,
        both,
        wide,
        both,
        both,
        both,
        wide,
        both,
        wide,
        both,
    )
    return jax.shard_map(
        per_device, mesh=mesh, in_specs=in_specs, out_specs=out_specs, check_vma=False
    )
```
